128 devices in a mesh: fsdp: 32 (over z, x, core), layer: 4 (over y).
Axes of the slice: x: 4, y: 4, z: 4, core: 2. Of those that a mesh axis runs over, the one named last changes fastest.
Arguments:
- gradients: bfloat16 [4, 256, 256, 256], P('layer', 'fsdp'), may hold values from -8 to 8
- second_moment: float32 [4, 256, 256, 256], P('layer', 'fsdp'), may hold values from 0.0001 to 0.01
- owners: int32 [4, 256, 1], P('layer'), may hold values from 0 to 31, as said below
- left_stats: float32 [4, 384, 256, 256], P('layer', 'fsdp'), may hold values from -0.3 to 4.3, as said below
- right_stats: float32 [4, 384, 256, 256], P('layer', 'fsdp'), may hold values from -0.3 to 4.3, as said below
- left_root: bfloat16 [4, 384, 256, 256], P('layer', 'fsdp'), may hold values from -0.3 to 1.8
- right_root: bfloat16 [4, 384, 256, 256], P('layer', 'fsdp'), may hold values from -0.3 to 1.8
Outputs:
- update: bfloat16 [4, 256, 256, 256], P('layer', 'fsdp')
- new_left_stats: float32 [4, 384, 256, 256], P('layer', 'fsdp')
- new_right_stats: float32 [4, 384, 256, 256], P('layer', 'fsdp')
The draws below stay inside these ranges and needn't reach their ends.
Inputs may be any that keep to these rules, and one draw needn't show every extreme that they name: In the list of one matrix, the 8 blocks of one index of fsdp (blocks i * 8 to (i + 1) * 8 - 1) name distinct owners, and no owner is named more than 12 times; every owner keeps the statistics and roots of its k-th owned block (in list order) in its slot k, and slots past its count are unused. `left_stats`: Symmetric. `right_stats`: Symmetric.
All inputs are finite; a program needn't handle non-finite values.
Results may differ from the reference program's by a relative error of at most 0.0057.
Values may be sent and summed in bfloat16 or wider, within the bound.
A program may use at most 192 MiB of HBM per device.

```python
import math
import jax
import jax.numpy as jnp
from jax import lax

BS = 256
BLK_DEV = 8
CAP = 12
NB = 256
SLOTS = 384
MATS = 4
N_FSDP = 32


def symmetric_part(key, spread):
    raw_part = jax.random.uniform(key, (MATS, SLOTS, BS, BS), jnp.float32, -1.0, 1.0) * (spread / math.sqrt(BS))
    return (raw_part + jnp.swapaxes(raw_part, 2, 3)) * 0.5


def draw_gradients(key, part):
    key = jax.random.fold_in(key, 11)
    key_noise, key_rows, key_cols = jax.random.split(key, 3)
    block_pos = jnp.arange(NB, dtype=jnp.float32) / float(NB - 1)
    matrix_pos = jnp.arange(MATS, dtype=jnp.float32) / float(max(MATS - 1, 1))
    ramp_sq = (1.0 + 2.0 * block_pos)[None, :] * (1.0 + 2.0 * matrix_pos)[:, None]
    noise_draw = jnp.clip(jax.random.normal(key_noise, (MATS, NB, BS, BS), jnp.float32), -4.0, 4.0)
    row_scale = jnp.exp(jax.random.uniform(key_rows, (MATS, NB, BS, 1), jnp.float32) * math.log(10.0))
    col_scale = jnp.exp(jax.random.uniform(key_cols, (MATS, NB, 1, BS), jnp.float32) * math.log(10.0))
    values = 0.005 * jnp.sqrt(ramp_sq)[:, :, None, None] * row_scale * col_scale * noise_draw
    return values.astype(jnp.bfloat16)


def owner_list_one(key):
    key_perm, key_tilt = jax.random.split(key)
    order = jax.random.permutation(key_perm, N_FSDP).astype(jnp.int32)
    spare = CAP - BLK_DEV
    tilt = jax.random.randint(key_tilt, (N_FSDP // 2,), 0, spare + 1).astype(jnp.int32)
    tilt = tilt.at[0].set(spare)
    pair_counts = jnp.stack([BLK_DEV + tilt, BLK_DEV - tilt], axis=1).reshape(N_FSDP)
    listed = jnp.repeat(order, pair_counts, total_repeat_length=NB)
    return listed.reshape(BLK_DEV, N_FSDP).T.reshape(NB).astype(jnp.int32)


def draw_owners(key, part):
    key = jax.random.fold_in(key, 31)
    rows = [owner_list_one(jax.random.fold_in(key, matrix_index)) for matrix_index in range(MATS)]
    return jnp.stack(rows)[:, :, None].astype(jnp.int32)


def stats_matrix(key):
    key_diag, key_off = jax.random.split(key)
    diagonal = jnp.exp(jax.random.uniform(key_diag, (MATS, SLOTS, BS), jnp.float32) * math.log(4.0))
    return symmetric_part(key_off, 1.2) + diagonal[:, :, :, None] * jnp.eye(BS, dtype=jnp.float32)


def root_matrix(key):
    key_diag, key_off = jax.random.split(key)
    diagonal = 0.5 * jnp.exp(jax.random.uniform(key_diag, (MATS, SLOTS, BS), jnp.float32) * math.log(3.0))
    return (symmetric_part(key_off, 1.2) + diagonal[:, :, :, None] * jnp.eye(BS, dtype=jnp.float32)).astype(jnp.bfloat16)


def draw_left_stats(key, part):
    key = jax.random.fold_in(key, 21)
    return stats_matrix(key)


def draw_right_stats(key, part):
    key = jax.random.fold_in(key, 22)
    return stats_matrix(key)


def draw_left_root(key, part):
    key = jax.random.fold_in(key, 23)
    return root_matrix(key)


def draw_right_root(key, part):
    key = jax.random.fold_in(key, 24)
    return root_matrix(key)


def shard_levels(rng, shape, shards, least, top_value):
    level, own = 1.0, jax.random.fold_in(rng, 6)
    for dim, blocks in shards:
        heights = jnp.exp(jax.random.uniform(jax.random.fold_in(own, dim), (blocks,), jnp.float32, least / len(shards), top_value / len(shards)))
        level = level * jnp.repeat(heights, shape[dim] // blocks).reshape([-1 if axis == dim else 1 for axis in range(len(shape))])
    return level


def setup_inputs(seed: int = 0) -> dict:
    keys = jax.random.split(jax.random.key(seed), 8)
    gradients = draw_gradients(jax.random.fold_in(keys[7], 71), 0)
    second_moment = jnp.clip(jnp.exp(math.log(0.01) - 4.6051702 * jax.random.uniform(keys[1], (MATS, NB, BS, BS), jnp.float32) ** shard_levels(keys[1], (MATS, NB, BS, BS), ((0, 4), (1, 32)), -0.2, 0.2)), 0.0001, 0.01)
    owners = draw_owners(jax.random.fold_in(keys[7], 71), 0)
    left_stats = draw_left_stats(jax.random.fold_in(keys[7], 71), 0)
    right_stats = draw_right_stats(jax.random.fold_in(keys[7], 71), 0)
    left_root = draw_left_root(jax.random.fold_in(keys[7], 71), 0)
    right_root = draw_right_root(jax.random.fold_in(keys[7], 71), 0)
    return dict(gradients=gradients, second_moment=second_moment, owners=owners, left_stats=left_stats, right_stats=right_stats, left_root=left_root, right_root=right_root)


ADAM_EPS = 1e-08
DECAY_RATE = 0.95
UPDATE_RMS = 1.0
NORM_FLOOR = 1e-06

def reference(gradients, second_moment, owners, left_stats, right_stats, left_root, right_root):
    adam_dir = gradients.astype(jnp.float32) / (jnp.sqrt(second_moment) + ADAM_EPS)
    block_sq = lax.optimization_barrier(jnp.sum(adam_dir * adam_dir, axis=(2, 3)))
    global_sq = jnp.sum(block_sq)
    clip_factor = jnp.minimum(1.0, UPDATE_RMS / jnp.sqrt(global_sq / float(MATS * NB * BS * BS)))
    updates = []
    lefts = []
    rights = []
    for matrix_index in range(MATS):
        owner_list = owners[matrix_index, :, 0].astype(jnp.int32)
        owner_hot = (owner_list[:, None] == jnp.arange(N_FSDP, dtype=jnp.int32)[None, :]).astype(jnp.int32)
        earlier = jnp.cumsum(owner_hot, axis=0) - owner_hot
        slot_number = lax.optimization_barrier(jnp.sum(earlier * owner_hot, axis=1)).astype(jnp.int32)
        slot_index = (owner_list * CAP + slot_number).astype(jnp.int32)
        grad_block = gradients[matrix_index].astype(jnp.float32)
        gram_left = jnp.einsum('bij,bkj->bik', grad_block, grad_block)
        gram_right = jnp.einsum('bji,bjk->bik', grad_block, grad_block)
        decayed_left = DECAY_RATE * left_stats[matrix_index]
        decayed_right = DECAY_RATE * right_stats[matrix_index]
        lefts.append(decayed_left.at[slot_index].add((1.0 - DECAY_RATE) * gram_left))
        rights.append(decayed_right.at[slot_index].add((1.0 - DECAY_RATE) * gram_right))
        left_sel = jnp.take(left_root[matrix_index], slot_index, axis=0).astype(jnp.float32)
        right_sel = jnp.take(right_root[matrix_index], slot_index, axis=0).astype(jnp.float32)
        half_done = jnp.einsum('bij,bjk->bik', left_sel, grad_block).astype(jnp.bfloat16)
        preconditioned = jnp.einsum('bij,bjk->bik', half_done.astype(jnp.float32), right_sel).astype(jnp.bfloat16)
        pre_float = preconditioned.astype(jnp.float32)
        graft_ratio = jnp.sqrt(block_sq[matrix_index] / float(BS * BS)) / jnp.sqrt(lax.optimization_barrier(jnp.sum(pre_float * pre_float, axis=(1, 2))) / float(BS * BS) + NORM_FLOOR)
        updates.append((pre_float * (graft_ratio * clip_factor)[:, None, None]).astype(jnp.bfloat16))
    return (jnp.stack(updates), jnp.stack(lefts), jnp.stack(rights))
```

```python
import functools

import jax
import jax.numpy as jnp
from jax import lax
from jax.experimental import pallas as pl
from jax.experimental.pallas import tpu as pltpu
from jax.sharding import PartitionSpec as P

ADAM_EPS = 1e-08
DECAY_RATE = 0.95
UPDATE_RMS = 1.0
NORM_FLOOR = 1e-06

MESH = pl.DeviceIdType.MESH
RING = 4
CORES = 2
N = RING * RING * CORES
LAYERS = 4
BS = 256
BLOCKS = 8
NB = N * BLOCKS
CAP = 12
ROWS = 16
LANES = 128
GROUPS = 3
PER = CAP // GROUPS
MIB = 2**20


def hops(step):
    dz, dx, _ = step
    return min(dz, RING - dz) + min(dx, RING - dx)


STEPS = sorted(
    (
        (dz, dx, dc)
        for dz in range(RING)
        for dx in range(RING)
        for dc in range(CORES)
        if (dz, dx, dc) != (0, 0, 0)
    ),
    key=lambda step: -hops(step),
)


def partner(me, step):
    dz, dx, dc = step
    z, x, c = me // (RING * CORES), (me // CORES) % RING, me % CORES
    return ((z + dz) % RING * RING + (x + dx) % RING) * CORES + (c + dc) % CORES


def piece(ref, k):
    rows = pl.ds(pl.multiple_of((k // 2) * ROWS, ROWS), ROWS)
    return ref.at[:, k % 2, rows, :]


def wait_bytes(ref, sem):
    pltpu.make_async_copy(ref, ref, sem).wait()


def routed_kernel(
    take_ref, back_ref, grad_ref, second_ref, left_ref, right_ref,
    owned_ref, home_ref, norms_ref,
    grad, second, left, right, spread, outgo, answer, arrived, homing, sums, totals,
    load_sems, self_sems, send_sems, route_sems, recv_sems, sum_sems,
):
    me = lax.axis_index("fsdp")
    layer = lax.axis_index("layer")

    barrier = pltpu.get_barrier_semaphore()
    for step in STEPS:
        pl.semaphore_signal(
            barrier, inc=1, device_id={"fsdp": partner(me, step)}, device_id_type=MESH
        )
    for offset in range(1, LAYERS):
        pl.semaphore_signal(
            barrier,
            inc=1,
            device_id={"layer": (layer + offset) % LAYERS},
            device_id_type=MESH,
        )
    loads = [
        pltpu.make_async_copy(
            grad_ref.at[0, :, :, pl.ds(half * LANES, LANES)], grad.at[:, half], load_sems.at[half]
        )
        for half in range(2)
    ]
    loads.append(pltpu.make_async_copy(second_ref.at[0], second, load_sems.at[2]))
    loads.append(pltpu.make_async_copy(left_ref.at[0], left, load_sems.at[3]))
    loads.append(pltpu.make_async_copy(right_ref.at[0], right, load_sems.at[4]))
    for load in loads:
        load.start()
    spread[NB] = jnp.zeros((ROWS, LANES), jnp.bfloat16)
    loads[0].wait()
    loads[1].wait()
    pl.semaphore_wait(barrier, N - 1 + LAYERS - 1)

    def remote(src, dst, send_sem, recv_sem, target):
        copy = pltpu.make_async_remote_copy(
            src_ref=src,
            dst_ref=dst,
            send_sem=send_sem,
            recv_sem=recv_sem,
            device_id={"fsdp": target},
            device_id_type=MESH,
        )
        copy.start()

    my_blocks = pl.ds(me * BLOCKS, BLOCKS)
    for step in STEPS:
        target = partner(me, step)
        remote(piece(grad, target), spread.at[my_blocks], send_sems.at[0], recv_sems.at[0], target)
    own = pltpu.make_async_copy(piece(grad, me), spread.at[my_blocks], self_sems.at[0])
    own.start()

    loads[2].wait()

    def adam_block(b, total):
        row_sum = jnp.zeros((8, LANES), jnp.float32)
        for half in range(2):
            for quarter in range(4):
                rows = pl.ds(quarter * 64, 64)
                lanes = pl.ds(half * LANES, LANES)
                direction = grad[b, half, rows, :].astype(jnp.float32) / (
                    jnp.sqrt(second[b, rows, lanes]) + ADAM_EPS
                )
                row_sum += jnp.sum((direction * direction).reshape(8, 8, LANES), axis=0)
        block_sum = jnp.full((8, LANES), jnp.sum(row_sum), jnp.float32)
        norms_ref[b] = block_sum
        return total + block_sum

    sums[N - 1] = lax.fori_loop(0, BLOCKS, adam_block, jnp.zeros((8, LANES), jnp.float32))

    own.wait()
    wait_bytes(spread.at[pl.ds(0, NB - BLOCKS)], recv_sems.at[0])

    for group in range(GROUPS):

        def take(target, carry):
            for slot in range(PER):
                row = spread[take_ref[target * CAP + group * PER + slot]]
                outgo[group, target * PER + slot] = row
            return carry

        lax.fori_loop(0, N, take, 0)
        place = owned_ref.at[pl.ds(group * PER, PER)]
        for step in STEPS:
            target = partner(me, step)
            remote(
                outgo.at[group, pl.ds(target * PER, PER)],
                piece(place, me),
                send_sems.at[1],
                route_sems.at[group],
                target,
            )
        pltpu.make_async_copy(
            outgo.at[group, pl.ds(me * PER, PER)], piece(place, me), self_sems.at[1 + group]
        ).start()

    for index, step in enumerate(STEPS):
        remote(sums.at[N - 1], sums.at[index], send_sems.at[4], sum_sems.at[0], partner(me, step))

    loads[3].wait()
    loads[4].wait()
    for group in range(GROUPS):
        place = owned_ref.at[pl.ds(group * PER, PER)]
        wait_bytes(outgo.at[group, pl.ds(0, PER * (N - 1))], route_sems.at[group])
        pltpu.make_async_copy(
            outgo.at[group, pl.ds(me * PER, PER)], piece(place, me), self_sems.at[1 + group]
        ).wait()

        def precondition(index, carry):
            slot = group * PER + index
            block = jnp.concatenate([owned_ref[slot, 0], owned_ref[slot, 1]], axis=1)
            half_done = jnp.dot(
                left[slot], block, preferred_element_type=jnp.float32
            ).astype(jnp.bfloat16)
            full = jnp.dot(
                half_done, right[slot], preferred_element_type=jnp.float32
            ).astype(jnp.bfloat16)
            answer[slot, 0] = full[:, :LANES]
            answer[slot, 1] = full[:, LANES:]
            return carry

        lax.fori_loop(0, PER, precondition, 0)
        done = answer.at[pl.ds(group * PER, PER)]
        landing = arrived.at[pl.ds(me * CAP + group * PER, PER)]
        for step in STEPS:
            target = partner(me, step)
            remote(piece(done, target), landing, send_sems.at[2], recv_sems.at[1], target)
        pltpu.make_async_copy(piece(done, me), landing, self_sems.at[4]).start()

    wait_bytes(sums.at[pl.ds(0, N - 1)], sum_sems.at[0])
    totals[LAYERS - 1] = jnp.sum(sums[...], axis=0)
    for offset in range(1, LAYERS):
        pltpu.make_async_remote_copy(
            src_ref=totals.at[LAYERS - 1],
            dst_ref=totals.at[offset - 1],
            send_sem=send_sems.at[5],
            recv_sem=sum_sems.at[1],
            device_id={"layer": (layer + offset) % LAYERS},
            device_id_type=MESH,
        ).start()

    wait_bytes(arrived.at[pl.ds(0, CAP)], self_sems.at[4])
    wait_bytes(arrived.at[pl.ds(0, CAP * (N - 1))], recv_sems.at[1])

    def give(target, carry):
        for block in range(BLOCKS):
            homing[target * BLOCKS + block] = arrived[back_ref[target * BLOCKS + block]]
        return carry

    lax.fori_loop(0, N, give, 0)
    for step in STEPS:
        target = partner(me, step)
        remote(
            homing.at[pl.ds(target * BLOCKS, BLOCKS)],
            piece(home_ref, me),
            send_sems.at[3],
            recv_sems.at[2],
            target,
        )
    own = pltpu.make_async_copy(homing.at[my_blocks], piece(home_ref, me), self_sems.at[5])
    own.start()

    wait_bytes(totals.at[pl.ds(0, LAYERS - 1)], sum_sems.at[1])
    norms_ref[BLOCKS] = jnp.sum(totals[...], axis=0)
    own.wait()
    wait_bytes(homing.at[pl.ds(0, NB - BLOCKS)], recv_sems.at[2])
    wait_bytes(homing.at[pl.ds(0, NB - BLOCKS)], send_sems.at[3])
    wait_bytes(spread.at[pl.ds(0, NB - BLOCKS)], send_sems.at[0])
    wait_bytes(arrived.at[pl.ds(0, CAP * (N - 1))], send_sems.at[1])
    wait_bytes(arrived.at[pl.ds(0, CAP * (N - 1))], send_sems.at[2])
    wait_bytes(sums.at[pl.ds(0, N - 1)], send_sems.at[4])
    wait_bytes(totals.at[pl.ds(0, LAYERS - 1)], send_sems.at[5])


def routed(take_table, back_table, gradients, second_moment, left_root, right_root):
    bf16, f32 = jnp.bfloat16, jnp.float32
    smem = pl.BlockSpec(memory_space=pltpu.SMEM)
    vmem = pl.BlockSpec(memory_space=pltpu.VMEM)
    hbm = pl.BlockSpec(memory_space=pl.ANY)
    return pl.pallas_call(
        routed_kernel,
        out_shape=(
            jax.ShapeDtypeStruct((CAP, 2, BS, LANES), bf16),
            jax.ShapeDtypeStruct((BLOCKS, 2, BS, LANES), bf16),
            jax.ShapeDtypeStruct((BLOCKS + 1, 8, LANES), f32),
        ),
        in_specs=[smem, smem, hbm, hbm, hbm, hbm],
        out_specs=(vmem, vmem, vmem),
        scratch_shapes=[
            pltpu.VMEM((BLOCKS, 2, BS, LANES), bf16),
            pltpu.VMEM((BLOCKS, BS, BS), f32),
            pltpu.VMEM((CAP, BS, BS), bf16),
            pltpu.VMEM((CAP, BS, BS), bf16),
            pltpu.VMEM((NB + 1, ROWS, LANES), bf16),
            pltpu.VMEM((GROUPS, N * PER, ROWS, LANES), bf16),
            pltpu.VMEM((CAP, 2, BS, LANES), bf16),
            pltpu.VMEM((N * CAP, ROWS, LANES), bf16),
            pltpu.VMEM((NB, ROWS, LANES), bf16),
            pltpu.VMEM((N, 8, LANES), f32),
            pltpu.VMEM((LAYERS, 8, LANES), f32),
            pltpu.SemaphoreType.DMA((5,)),
            pltpu.SemaphoreType.DMA((6,)),
            pltpu.SemaphoreType.DMA((6,)),
            pltpu.SemaphoreType.DMA((GROUPS,)),
            pltpu.SemaphoreType.DMA((3,)),
            pltpu.SemaphoreType.DMA((2,)),
        ],
        compiler_params=pltpu.CompilerParams(
            collective_id=0, has_side_effects=True, vmem_limit_bytes=32 * MIB
        ),
        cost_estimate=pl.CostEstimate(
            flops=2 * 2 * CAP * BS**3, bytes_accessed=10 * MIB, transcendentals=0
        ),
        name="route_blocks",
    )(take_table, back_table, gradients, second_moment, left_root, right_root)


SLOTS_STEP = 3
BLOCKS_STEP = 2


def finish_kernel(owned_ref, home_ref, norms_ref, total_ref, left_ref, right_ref,
                  update_ref, new_left_ref, new_right_ref):
    for slot in range(SLOTS_STEP):
        block = jnp.concatenate([owned_ref[slot, 0], owned_ref[slot, 1]], axis=1)
        gram_left = lax.dot_general(
            block, block, (((1,), (1,)), ((), ())), preferred_element_type=jnp.float32
        )
        gram_right = lax.dot_general(
            block, block, (((0,), (0,)), ((), ())), preferred_element_type=jnp.float32
        )
        new_left_ref[0, slot] = DECAY_RATE * left_ref[0, slot] + (1.0 - DECAY_RATE) * gram_left
        new_right_ref[0, slot] = DECAY_RATE * right_ref[0, slot] + (1.0 - DECAY_RATE) * gram_right
    entries = float(LAYERS * NB * BS * BS)
    clip_factor = jnp.minimum(1.0, UPDATE_RMS / jnp.sqrt(total_ref[0, :1, :] / entries))
    for block in range(BLOCKS_STEP):
        pre = home_ref[block].astype(jnp.float32)
        pre_sq = jnp.full((1, LANES), jnp.sum(pre * pre), jnp.float32)
        ratio = jnp.sqrt(norms_ref[block, :1, :] / float(BS * BS)) / jnp.sqrt(
            pre_sq / float(BS * BS) + NORM_FLOOR
        )
        factor = ratio * clip_factor
        for half in range(2):
            update_ref[0, block, :, half * LANES : (half + 1) * LANES] = (
                pre[half] * factor
            ).astype(jnp.bfloat16)


def finish(owned, home, norms, left_stats, right_stats):
    def slots(*tail):
        return pl.BlockSpec((1, SLOTS_STEP) + tail, lambda i: (0, i, 0, 0))

    def blocks(n, *tail):
        return pl.BlockSpec((n,) + tail, lambda i: (i,) + (0,) * len(tail))

    return pl.pallas_call(
        finish_kernel,
        grid=(CAP // SLOTS_STEP,),
        out_shape=(
            jax.ShapeDtypeStruct((1, BLOCKS, BS, BS), jnp.bfloat16),
            jax.ShapeDtypeStruct((1, CAP, BS, BS), jnp.float32),
            jax.ShapeDtypeStruct((1, CAP, BS, BS), jnp.float32),
        ),
        in_specs=[
            blocks(SLOTS_STEP, 2, BS, LANES),
            blocks(BLOCKS_STEP, 2, BS, LANES),
            blocks(BLOCKS_STEP, 8, LANES),
            pl.BlockSpec((1, 8, LANES), lambda i: (BLOCKS, 0, 0)),
            slots(BS, BS),
            slots(BS, BS),
        ],
        out_specs=(
            pl.BlockSpec((1, BLOCKS_STEP, BS, BS), lambda i: (0, i, 0, 0)),
            slots(BS, BS),
            slots(BS, BS),
        ),
        compiler_params=pltpu.CompilerParams(vmem_limit_bytes=24 * MIB),
        cost_estimate=pl.CostEstimate(
            flops=2 * 2 * CAP * BS**3, bytes_accessed=16 * MIB, transcendentals=0
        ),
        name="finish_stats",
    )(owned, home, norms, norms, left_stats, right_stats)


def slot_tables(owner_list):
    rows = lax.iota(jnp.int32, NB)
    same = owner_list[:, None] == owner_list[None, :]
    earlier = jnp.sum((same & (rows[:, None] > rows[None, :])).astype(jnp.int32), axis=1)
    slot_index = owner_list * CAP + earlier
    hit = lax.iota(jnp.int32, N * CAP)[:, None] == slot_index[None, :]
    take = NB + jnp.sum(jnp.where(hit, rows[None, :] - NB, 0), axis=1)
    return take, slot_index


def per_device(gradients, second_moment, owners, left_stats, right_stats, left_root, right_root):
    take_table, back_table = slot_tables(owners[0, :, 0])
    owned, home, norms = routed(
        take_table, back_table, gradients, second_moment, left_root, right_root
    )
    return finish(owned, home, norms, left_stats, right_stats)


def solution(mesh):
    blocked = P("layer", "fsdp", None, None)
    return jax.shard_map(
        per_device,
        mesh=mesh,
        in_specs=(blocked, blocked, P("layer", None, None), blocked, blocked, blocked, blocked),
        out_specs=(blocked, blocked, blocked),
        check_vma=False,
    )
```

```python
import jax
import jax.numpy as jnp
from jax import lax
from jax.experimental import pallas as pl
from jax.experimental.pallas import tpu as pltpu
from jax.sharding import PartitionSpec as P

ADAM_EPS = 1e-08
DECAY_RATE = 0.95
UPDATE_RMS = 1.0
NORM_FLOOR = 1e-06

MESH = pl.DeviceIdType.MESH
RING = 4
CORES = 2
N = RING * RING * CORES
LAYERS = 4
BS = 256
BLOCKS = 8
NB = N * BLOCKS
CAP = 12
ROWS = 16
LANES = 128
GROUPS = 3
PER = CAP // GROUPS
MIB = 2**20


def hops(step):
    dz, dx, _ = step
    return min(dz, RING - dz) + min(dx, RING - dx)


STEPS = sorted(
    (
        (dz, dx, dc)
        for dz in range(RING)
        for dx in range(RING)
        for dc in range(CORES)
        if (dz, dx, dc) != (0, 0, 0)
    ),
    key=lambda step: (-hops(step), step[2], min(step[0], RING - step[0]), step),
)


def partner(me, step):
    dz, dx, dc = step
    z, x, c = me // (RING * CORES), (me // CORES) % RING, me % CORES
    return ((z + dz) % RING * RING + (x + dx) % RING) * CORES + (c + dc) % CORES


def by_core(me):
    z, x = me // (RING * CORES), (me // CORES) % RING
    places = [step[:2] for step in STEPS if step[2] == 0]

    def on_core(core):
        return [((z + dz) % RING * RING + (x + dx) % RING) * CORES + core for dz, dx in places]

    return on_core(0) + [partner(me, (0, 0, 1))] + on_core(1)


def piece_place(k):
    if isinstance(k, int):
        return pl.ds((k // 2) * ROWS, ROWS), pl.ds((k % 2) * LANES, LANES)
    rows = pl.ds(pl.multiple_of((k // 2) * ROWS, ROWS), ROWS)
    return rows, pl.ds(pl.multiple_of((k % 2) * LANES, LANES), LANES)


def join(pieces):
    return jnp.concatenate(
        [
            jnp.concatenate([pieces(2 * r + half) for r in range(BS // ROWS)], axis=0)
            for half in range(2)
        ],
        axis=1,
    )


def wait_bytes(ref, sem):
    pltpu.make_async_copy(ref, ref, sem).wait()


def slot_tables(owner_row):
    rows = lax.broadcasted_iota(jnp.int32, (NB, NB), 0)
    columns = lax.broadcasted_iota(jnp.int32, (NB, NB), 1)

    def upright(row):
        return jnp.sum(jnp.where(rows == columns, row, 0), axis=1, keepdims=True)

    same = (upright(owner_row) == owner_row) & (rows < columns)
    slot_index = owner_row * CAP + jnp.sum(jnp.where(same, 1, 0), axis=0, keepdims=True)
    slots = lax.broadcasted_iota(jnp.int32, (NB, N * CAP), 1)
    blocks = lax.broadcasted_iota(jnp.int32, (NB, N * CAP), 0)
    hit = upright(slot_index) == slots
    taken = NB + jnp.sum(jnp.where(hit, blocks - NB, 0), axis=0, keepdims=True)
    return taken, slot_index


def routed_kernel(
    owner_ref, grad_ref, second_ref, left_root_ref, right_root_ref, left_stats_ref, right_stats_ref,
    new_left_ref, new_right_ref, home_ref, norms_ref,
    owner_row, grad, second, left_root, right_root, left_stats, right_stats,
    leaving, spread, outgo, landed, owned, answer, arrived, homing, sums, totals,
    take_rows, back_rows, take_table, back_table,
    load_sems, table_sems, send_sems, route_sems, recv_sems, sum_sems,
):
    me = lax.axis_index("fsdp")
    layer = lax.axis_index("layer")

    barrier = pltpu.get_barrier_semaphore()
    for step in STEPS:
        pl.semaphore_signal(
            barrier, inc=1, device_id={"fsdp": partner(me, step)}, device_id_type=MESH
        )
    for offset in range(1, LAYERS):
        pl.semaphore_signal(
            barrier,
            inc=1,
            device_id={"layer": (layer + offset) % LAYERS},
            device_id_type=MESH,
        )
    loads = [
        pltpu.make_async_copy(src, dst, load_sems.at[index])
        for index, (src, dst) in enumerate(
            (
                (grad_ref.at[0], grad),
                (owner_ref, owner_row),
                (second_ref.at[0], second),
                (left_root_ref.at[0], left_root),
                (right_root_ref.at[0], right_root),
                (left_stats_ref.at[0], left_stats),
                (right_stats_ref.at[0], right_stats),
            )
        )
    ]
    loads[0].start()
    loads[1].start()
    loads[0].wait()
    pl.semaphore_wait(barrier, N - 1 + LAYERS - 1)

    def remote(src, dst, send_sem, recv_sem, target):
        copy = pltpu.make_async_remote_copy(
            src_ref=src,
            dst_ref=dst,
            send_sem=send_sem,
            recv_sem=recv_sem,
            device_id={"fsdp": target},
            device_id_type=MESH,
        )
        copy.start()

    targets = [partner(me, step) for step in STEPS]
    my_blocks = pl.ds(me * BLOCKS, BLOCKS)

    for target in by_core(me):
        leaving[target] = grad[(slice(None),) + piece_place(target)]
        remote(
            leaving.at[target], spread.at[my_blocks], send_sems.at[0], recv_sems.at[0], target
        )
    spread[my_blocks] = grad[(slice(None),) + piece_place(me)]
    spread[NB] = jnp.zeros((ROWS, LANES), jnp.bfloat16)

    for load in loads[2:]:
        load.start()
    loads[1].wait()
    take_rows[...], back_rows[...] = slot_tables(owner_row[...])
    tables = [
        pltpu.make_async_copy(take_rows, take_table, table_sems.at[0]),
        pltpu.make_async_copy(back_rows, back_table, table_sems.at[1]),
    ]
    for table in tables:
        table.start()
    for table in tables:
        table.wait()
    wait_bytes(spread.at[pl.ds(0, NB - BLOCKS)], recv_sems.at[0])

    def take(ref, group, target):
        for slot in range(PER):
            ref[group, target, slot] = spread[take_table[0, target * CAP + group * PER + slot]]

    for group in range(GROUPS):
        for target in targets:
            take(outgo, group, target)
            remote(
                outgo.at[group, target],
                landed.at[group, me],
                send_sems.at[1],
                route_sems.at[group],
                target,
            )
        take(landed, group, me)

    loads[3].wait()
    loads[4].wait()
    for group in range(GROUPS):
        wait_bytes(landed.at[group, pl.ds(0, N - 1)], route_sems.at[group])

        def precondition(index, carry):
            slot = group * PER + index
            block = join(lambda k: landed[group, k, index])
            owned[slot] = block
            half_done = jnp.dot(
                left_root[slot], block, preferred_element_type=jnp.float32
            ).astype(jnp.bfloat16)
            full = jnp.dot(
                half_done, right_root[slot], preferred_element_type=jnp.float32
            ).astype(jnp.bfloat16)
            for k in range(N):
                r, half = divmod(k, 2)
                answer[group, k, index] = full[
                    r * ROWS : (r + 1) * ROWS, half * LANES : (half + 1) * LANES
                ]
            return carry

        lax.fori_loop(0, PER, precondition, 0)
        landing = pl.ds(me * CAP + group * PER, PER)
        for target in by_core(me):
            remote(
                answer.at[group, target],
                arrived.at[landing],
                send_sems.at[2],
                recv_sems.at[1],
                target,
            )
        arrived[landing] = answer[group, me]

    loads[2].wait()

    def adam_block(b, total):
        row_sum = jnp.zeros((8, LANES), jnp.float32)
        for half in range(2):
            for quarter in range(4):
                rows = pl.ds(quarter * 64, 64)
                lanes = pl.ds(half * LANES, LANES)
                direction = grad[b, rows, lanes].astype(jnp.float32) / (
                    jnp.sqrt(second[b, rows, lanes]) + ADAM_EPS
                )
                row_sum += jnp.sum((direction * direction).reshape(8, 8, LANES), axis=0)
        block_sum = jnp.full((8, LANES), jnp.sum(row_sum), jnp.float32)
        norms_ref[b] = block_sum
        return total + block_sum

    sums[N - 1] = lax.fori_loop(0, BLOCKS, adam_block, jnp.zeros((8, LANES), jnp.float32))

    for index, target in enumerate(targets):
        remote(sums.at[N - 1], sums.at[index], send_sems.at[4], sum_sems.at[0], target)

    wait_bytes(arrived.at[pl.ds(0, CAP * (N - 1))], recv_sems.at[1])

    def give(ref, target):
        for block in range(BLOCKS):
            ref[target, block] = arrived[back_table[0, target * BLOCKS + block]]

    for target in targets:
        give(homing, target)
        remote(homing.at[target], home_ref.at[me], send_sems.at[3], recv_sems.at[2], target)
    give(home_ref, me)

    loads[5].wait()
    loads[6].wait()

    def statistics(slot, carry):
        block = owned[slot]
        gram_left = lax.dot_general(
            block, block, (((1,), (1,)), ((), ())), preferred_element_type=jnp.float32
        )
        gram_right = lax.dot_general(
            block, block, (((0,), (0,)), ((), ())), preferred_element_type=jnp.float32
        )
        new_left_ref[slot] = DECAY_RATE * left_stats[slot] + (1.0 - DECAY_RATE) * gram_left
        new_right_ref[slot] = DECAY_RATE * right_stats[slot] + (1.0 - DECAY_RATE) * gram_right
        return carry

    lax.fori_loop(0, CAP // 2, statistics, 0)

    wait_bytes(sums.at[pl.ds(0, N - 1)], sum_sems.at[0])
    totals[LAYERS - 1] = jnp.sum(sums[...], axis=0)
    for offset in range(1, LAYERS):
        pltpu.make_async_remote_copy(
            src_ref=totals.at[LAYERS - 1],
            dst_ref=totals.at[offset - 1],
            send_sem=send_sems.at[5],
            recv_sem=sum_sems.at[1],
            device_id={"layer": (layer + offset) % LAYERS},
            device_id_type=MESH,
        ).start()
    lax.fori_loop(CAP // 2, CAP, statistics, 0)

    wait_bytes(totals.at[pl.ds(0, LAYERS - 1)], sum_sems.at[1])
    norms_ref[BLOCKS] = jnp.sum(totals[...], axis=0)
    wait_bytes(leaving.at[pl.ds(0, N - 1)], send_sems.at[0])
    wait_bytes(arrived.at[pl.ds(0, CAP * (N - 1))], send_sems.at[1])
    wait_bytes(arrived.at[pl.ds(0, CAP * (N - 1))], send_sems.at[2])
    wait_bytes(sums.at[pl.ds(0, N - 1)], send_sems.at[4])
    wait_bytes(totals.at[pl.ds(0, LAYERS - 1)], send_sems.at[5])
    wait_bytes(homing.at[pl.ds(0, N - 1)], send_sems.at[3])
    wait_bytes(home_ref.at[pl.ds(0, N - 1)], recv_sems.at[2])


def routed(owner_row, gradients, second_moment, left_root, right_root, left_stats, right_stats):
    bf16, f32 = jnp.bfloat16, jnp.float32
    vmem = pl.BlockSpec(memory_space=pltpu.VMEM)
    hbm = pl.BlockSpec(memory_space=pltpu.HBM)
    operands = [
        pltpu.with_memory_space_constraint(array, pltpu.HBM)
        for array in (
            owner_row, gradients, second_moment, left_root, right_root, left_stats, right_stats
        )
    ]
    return pl.pallas_call(
        routed_kernel,
        out_shape=(
            pltpu.VMEM((CAP, BS, BS), f32),
            pltpu.VMEM((CAP, BS, BS), f32),
            pltpu.VMEM((N, BLOCKS, ROWS, LANES), bf16),
            pltpu.VMEM((BLOCKS + 1, 8, LANES), f32),
        ),
        in_specs=[hbm] * len(operands),
        out_specs=(vmem,) * 4,
        scratch_shapes=[
            pltpu.VMEM((1, NB), jnp.int32),
            pltpu.VMEM((BLOCKS, BS, BS), bf16),
            pltpu.VMEM((BLOCKS, BS, BS), f32),
            pltpu.VMEM((CAP, BS, BS), bf16),
            pltpu.VMEM((CAP, BS, BS), bf16),
            pltpu.VMEM((CAP, BS, BS), f32),
            pltpu.VMEM((CAP, BS, BS), f32),
            pltpu.VMEM((N, BLOCKS, ROWS, LANES), bf16),
            pltpu.VMEM((NB + 1, ROWS, LANES), bf16),
            pltpu.VMEM((GROUPS, N, PER, ROWS, LANES), bf16),
            pltpu.VMEM((GROUPS, N, PER, ROWS, LANES), bf16),
            pltpu.VMEM((CAP, BS, BS), bf16),
            pltpu.VMEM((GROUPS, N, PER, ROWS, LANES), bf16),
            pltpu.VMEM((N * CAP, ROWS, LANES), bf16),
            pltpu.VMEM((N, BLOCKS, ROWS, LANES), bf16),
            pltpu.VMEM((N, 8, LANES), f32),
            pltpu.VMEM((LAYERS, 8, LANES), f32),
            pltpu.VMEM((1, N * CAP), jnp.int32),
            pltpu.VMEM((1, NB), jnp.int32),
            pltpu.SMEM((1, N * CAP), jnp.int32),
            pltpu.SMEM((1, NB), jnp.int32),
            pltpu.SemaphoreType.DMA((7,)),
            pltpu.SemaphoreType.DMA((2,)),
            pltpu.SemaphoreType.DMA((6,)),
            pltpu.SemaphoreType.DMA((GROUPS,)),
            pltpu.SemaphoreType.DMA((3,)),
            pltpu.SemaphoreType.DMA((2,)),
        ],
        compiler_params=pltpu.CompilerParams(
            collective_id=0, has_side_effects=True, vmem_limit_bytes=34 * MIB
        ),
        cost_estimate=pl.CostEstimate(
            flops=4 * 2 * CAP * BS**3, bytes_accessed=18 * MIB, transcendentals=0
        ),
        name="route_blocks",
    )(*operands)


def finish_kernel(left_ref, right_ref, home_ref, norms_ref,
                  update_ref, new_left_ref, new_right_ref, update, sems):
    outs = [
        pltpu.make_async_copy(left_ref, new_left_ref.at[0], sems.at[0]),
        pltpu.make_async_copy(right_ref, new_right_ref.at[0], sems.at[1]),
    ]
    for out in outs:
        out.start()
    entries = float(LAYERS * NB * BS * BS)
    clip_factor = jnp.minimum(1.0, UPDATE_RMS / jnp.sqrt(norms_ref[BLOCKS, :1, :] / entries))
    for block in range(BLOCKS):
        pre = home_ref[:, block].astype(jnp.float32)
        pre_sq = jnp.full((1, LANES), jnp.sum(pre * pre), jnp.float32)
        ratio = jnp.sqrt(norms_ref[block, :1, :] / float(BS * BS)) / jnp.sqrt(
            pre_sq / float(BS * BS) + NORM_FLOOR
        )
        factor = ratio * clip_factor
        for k in range(N):
            update[(block,) + piece_place(k)] = (pre[k] * factor).astype(jnp.bfloat16)
    out = pltpu.make_async_copy(update, update_ref.at[0], sems.at[2])
    out.start()
    for copy in outs + [out]:
        copy.wait()


def finish(new_left, new_right, home, norms):
    vmem = pl.BlockSpec(memory_space=pltpu.VMEM)
    hbm = pl.BlockSpec(memory_space=pltpu.HBM)
    return pl.pallas_call(
        finish_kernel,
        out_shape=(
            jax.ShapeDtypeStruct((1, BLOCKS, BS, BS), jnp.bfloat16),
            jax.ShapeDtypeStruct((1, CAP, BS, BS), jnp.float32),
            jax.ShapeDtypeStruct((1, CAP, BS, BS), jnp.float32),
        ),
        in_specs=[vmem] * 4,
        out_specs=(hbm,) * 3,
        scratch_shapes=[
            pltpu.VMEM((BLOCKS, BS, BS), jnp.bfloat16),
            pltpu.SemaphoreType.DMA((3,)),
        ],
        compiler_params=pltpu.CompilerParams(vmem_limit_bytes=8 * MIB),
        cost_estimate=pl.CostEstimate(
            flops=6 * BLOCKS * BS * BS, bytes_accessed=14 * MIB, transcendentals=0
        ),
        name="write_results",
    )(new_left, new_right, home, norms)


def per_device(gradients, second_moment, owners, left_stats, right_stats, left_root, right_root):
    owner_row = owners.reshape(1, NB)
    new_left, new_right, home, norms = routed(
        owner_row, gradients, second_moment, left_root, right_root, left_stats, right_stats
    )
    return finish(new_left, new_right, home, norms)


def solution(mesh):
    blocked = P("layer", "fsdp", None, None)
    return jax.shard_map(
        per_device,
        mesh=mesh,
        in_specs=(blocked, blocked, P("layer", None, None), blocked, blocked, blocked, blocked),
        out_specs=(blocked, blocked, blocked),
        check_vma=False,
    )
```

```python
import jax
import jax.numpy as jnp
from jax import lax
from jax.experimental import pallas as pl
from jax.experimental.pallas import tpu as pltpu
from jax.sharding import PartitionSpec as P

ADAM_EPS = 1e-08
DECAY_RATE = 0.95
UPDATE_RMS = 1.0
NORM_FLOOR = 1e-06

MESH = pl.DeviceIdType.MESH
RING = 4
CORES = 2
N = RING * RING * CORES
LAYERS = 4
BS = 256
BLOCKS = 8
NB = N * BLOCKS
CAP = 12
ROWS = 16
LANES = 128
GROUPS = 3
PER = CAP // GROUPS
MIB = 2**20


def hops(step):
    dz, dx, _ = step
    return min(dz, RING - dz) + min(dx, RING - dx)


STEPS = sorted(
    (
        (dz, dx, dc)
        for dz in range(RING)
        for dx in range(RING)
        for dc in range(CORES)
        if (dz, dx, dc) != (0, 0, 0)
    ),
    key=lambda step: (-hops(step), step[2], min(step[0], RING - step[0]), step),
)


def partner(me, step):
    dz, dx, dc = step
    z, x, c = me // (RING * CORES), (me // CORES) % RING, me % CORES
    return ((z + dz) % RING * RING + (x + dx) % RING) * CORES + (c + dc) % CORES


def by_core(me):
    z, x = me // (RING * CORES), (me // CORES) % RING
    places = [step[:2] for step in STEPS if step[2] == 0]

    def on_core(core):
        return [((z + dz) % RING * RING + (x + dx) % RING) * CORES + core for dz, dx in places]

    return on_core(0), on_core(1)


def piece_place(k):
    if isinstance(k, int):
        return pl.ds((k // 2) * ROWS, ROWS), pl.ds((k % 2) * LANES, LANES)
    rows = pl.ds(pl.multiple_of((k // 2) * ROWS, ROWS), ROWS)
    return rows, pl.ds(pl.multiple_of((k % 2) * LANES, LANES), LANES)


def join(pieces):
    return jnp.concatenate(
        [
            jnp.concatenate([pieces(2 * r + half) for r in range(BS // ROWS)], axis=0)
            for half in range(2)
        ],
        axis=1,
    )


def wait_bytes(ref, sem):
    pltpu.make_async_copy(ref, ref, sem).wait()


def slot_tables(owner_row):
    rows = lax.broadcasted_iota(jnp.int32, (NB, NB), 0)
    columns = lax.broadcasted_iota(jnp.int32, (NB, NB), 1)

    def upright(row):
        return jnp.sum(jnp.where(rows == columns, row, 0), axis=1, keepdims=True)

    same = (upright(owner_row) == owner_row) & (rows < columns)
    slot_index = owner_row * CAP + jnp.sum(jnp.where(same, 1, 0), axis=0, keepdims=True)
    slots = lax.broadcasted_iota(jnp.int32, (NB, N * CAP), 1)
    blocks = lax.broadcasted_iota(jnp.int32, (NB, N * CAP), 0)
    hit = upright(slot_index) == slots
    taken = NB + jnp.sum(jnp.where(hit, blocks - NB, 0), axis=0, keepdims=True)
    return taken, slot_index


def routed_kernel(
    owner_ref, grad_ref, second_ref, left_root_ref, right_root_ref, left_stats_ref, right_stats_ref,
    new_left_ref, new_right_ref, home_ref, norms_ref,
    owner_row, grad, second, left_root, right_root, left_stats, right_stats,
    leaving, spread, outgo, landed, owned, answer, arrived, homing, sums, totals,
    take_rows, back_rows, take_table, back_table,
    load_sems, table_sems, send_sems, route_sems, recv_sems, sum_sems,
):
    me = lax.axis_index("fsdp")
    layer = lax.axis_index("layer")

    barrier = pltpu.get_barrier_semaphore()
    for step in STEPS:
        pl.semaphore_signal(
            barrier, inc=1, device_id={"fsdp": partner(me, step)}, device_id_type=MESH
        )
    for offset in range(1, LAYERS):
        pl.semaphore_signal(
            barrier,
            inc=1,
            device_id={"layer": (layer + offset) % LAYERS},
            device_id_type=MESH,
        )
    loads = [
        pltpu.make_async_copy(src, dst, load_sems.at[index])
        for index, (src, dst) in enumerate(
            (
                (grad_ref.at[0], grad),
                (owner_ref, owner_row),
                (second_ref.at[0], second),
                (left_root_ref.at[0], left_root),
                (right_root_ref.at[0], right_root),
                (left_stats_ref.at[0], left_stats),
                (right_stats_ref.at[0], right_stats),
            )
        )
    ]
    loads[0].start()
    loads[1].start()
    loads[0].wait()
    pl.semaphore_wait(barrier, N - 1 + LAYERS - 1)

    def remote(src, dst, send_sem, recv_sem, target):
        copy = pltpu.make_async_remote_copy(
            src_ref=src,
            dst_ref=dst,
            send_sem=send_sem,
            recv_sem=recv_sem,
            device_id={"fsdp": target},
            device_id_type=MESH,
        )
        copy.start()

    targets = [partner(me, step) for step in STEPS]
    my_blocks = pl.ds(me * BLOCKS, BLOCKS)

    to_core = by_core(me)
    sibling = partner(me, (0, 0, 1))
    for target in to_core[0] + [sibling] + to_core[1]:
        leaving[target] = grad[(slice(None),) + piece_place(target)]
        remote(
            leaving.at[target], spread.at[my_blocks], send_sems.at[0], recv_sems.at[0], target
        )
    spread[my_blocks] = grad[(slice(None),) + piece_place(me)]
    spread[NB] = jnp.zeros((ROWS, LANES), jnp.bfloat16)

    for load in loads[2:]:
        load.start()
    loads[1].wait()
    take_rows[...], back_rows[...] = slot_tables(owner_row[...])
    tables = [
        pltpu.make_async_copy(take_rows, take_table, table_sems.at[0]),
        pltpu.make_async_copy(back_rows, back_table, table_sems.at[1]),
    ]
    for table in tables:
        table.start()
    loads[2].wait()

    def adam_block(b, total):
        row_sum = jnp.zeros((8, LANES), jnp.float32)
        for half in range(2):
            for quarter in range(4):
                rows = pl.ds(quarter * 64, 64)
                lanes = pl.ds(half * LANES, LANES)
                direction = grad[b, rows, lanes].astype(jnp.float32) / (
                    jnp.sqrt(second[b, rows, lanes]) + ADAM_EPS
                )
                row_sum += jnp.sum((direction * direction).reshape(8, 8, LANES), axis=0)
        block_sum = jnp.full((1, LANES), jnp.sum(row_sum), jnp.float32)
        norms_ref[b] = block_sum
        return total + block_sum

    sums[N - 1] = lax.fori_loop(0, BLOCKS, adam_block, jnp.zeros((1, LANES), jnp.float32))

    for table in tables:
        table.wait()
    wait_bytes(spread.at[pl.ds(0, NB - BLOCKS)], recv_sems.at[0])

    def take(ref, group, target):
        for slot in range(PER):
            ref[group, target, slot] = spread[take_table[0, target * CAP + group * PER + slot]]

    for group in range(GROUPS):
        for target in targets:
            take(outgo, group, target)
            remote(
                outgo.at[group, target],
                landed.at[group, me],
                send_sems.at[1],
                route_sems.at[group],
                target,
            )
        take(landed, group, me)

    for index, target in enumerate(targets):
        remote(sums.at[N - 1], sums.at[index], send_sems.at[4], sum_sems.at[0], target)

    loads[3].wait()
    loads[4].wait()
    def send_answers(group, core):
        landing = pl.ds(me * CAP + group * PER, PER)
        for target in to_core[core] + ([sibling] if core == 0 else []):
            remote(
                answer.at[group, target],
                arrived.at[landing],
                send_sems.at[2],
                recv_sems.at[1],
                target,
            )
        if core == 0:
            arrived[landing] = answer[group, me]

    for group in range(GROUPS):
        wait_bytes(landed.at[group, pl.ds(0, N - 1)], route_sems.at[group])
        if group > 0:
            send_answers(group - 1, 0)

        def precondition(index, carry):
            slot = group * PER + index
            block = join(lambda k: landed[group, k, index])
            owned[slot] = block
            half_done = jnp.dot(
                left_root[slot], block, preferred_element_type=jnp.float32
            ).astype(jnp.bfloat16)
            full = jnp.dot(
                half_done, right_root[slot], preferred_element_type=jnp.float32
            ).astype(jnp.bfloat16)
            for k in range(N):
                r, half = divmod(k, 2)
                answer[group, k, index] = full[
                    r * ROWS : (r + 1) * ROWS, half * LANES : (half + 1) * LANES
                ]
            return carry

        lax.fori_loop(0, PER, precondition, 0)

    send_answers(GROUPS - 1, 0)
    for group in range(GROUPS):
        send_answers(group, 1)

    wait_bytes(sums.at[pl.ds(0, N - 1)], sum_sems.at[0])
    totals[LAYERS - 1] = jnp.sum(sums[...], axis=0)
    for offset in range(1, LAYERS):
        pltpu.make_async_remote_copy(
            src_ref=totals.at[LAYERS - 1],
            dst_ref=totals.at[offset - 1],
            send_sem=send_sems.at[5],
            recv_sem=sum_sems.at[1],
            device_id={"layer": (layer + offset) % LAYERS},
            device_id_type=MESH,
        ).start()

    wait_bytes(arrived.at[pl.ds(0, CAP * (N - 1))], recv_sems.at[1])

    def give(ref, target):
        for block in range(BLOCKS):
            ref[target, block] = arrived[back_table[0, target * BLOCKS + block]]

    for target in targets:
        give(homing, target)
        remote(homing.at[target], home_ref.at[me], send_sems.at[3], recv_sems.at[2], target)
    give(home_ref, me)

    loads[5].wait()
    loads[6].wait()

    def statistics(slot, carry):
        block = owned[slot]
        gram_left = lax.dot_general(
            block, block, (((1,), (1,)), ((), ())), preferred_element_type=jnp.float32
        )
        gram_right = lax.dot_general(
            block, block, (((0,), (0,)), ((), ())), preferred_element_type=jnp.float32
        )
        new_left_ref[slot] = DECAY_RATE * left_stats[slot] + (1.0 - DECAY_RATE) * gram_left
        new_right_ref[slot] = DECAY_RATE * right_stats[slot] + (1.0 - DECAY_RATE) * gram_right
        return carry

    lax.fori_loop(0, CAP, statistics, 0)


    wait_bytes(totals.at[pl.ds(0, LAYERS - 1)], sum_sems.at[1])
    norms_ref[BLOCKS] = jnp.sum(totals[...], axis=0)
    wait_bytes(leaving.at[pl.ds(0, N - 1)], send_sems.at[0])
    wait_bytes(arrived.at[pl.ds(0, CAP * (N - 1))], send_sems.at[1])
    wait_bytes(arrived.at[pl.ds(0, CAP * (N - 1))], send_sems.at[2])
    wait_bytes(sums.at[pl.ds(0, N - 1)], send_sems.at[4])
    wait_bytes(totals.at[pl.ds(0, LAYERS - 1)], send_sems.at[5])
    wait_bytes(homing.at[pl.ds(0, N - 1)], send_sems.at[3])
    wait_bytes(home_ref.at[pl.ds(0, N - 1)], recv_sems.at[2])


def routed(owner_row, gradients, second_moment, left_root, right_root, left_stats, right_stats):
    bf16, f32 = jnp.bfloat16, jnp.float32
    vmem = pl.BlockSpec(memory_space=pltpu.VMEM)
    hbm = pl.BlockSpec(memory_space=pltpu.HBM)
    operands = [
        pltpu.with_memory_space_constraint(array, pltpu.HBM)
        for array in (
            owner_row, gradients, second_moment, left_root, right_root, left_stats, right_stats
        )
    ]
    return pl.pallas_call(
        routed_kernel,
        out_shape=(
            pltpu.VMEM((CAP, BS, BS), f32),
            pltpu.VMEM((CAP, BS, BS), f32),
            pltpu.VMEM((N, BLOCKS, ROWS, LANES), bf16),
            pltpu.VMEM((BLOCKS + 1, 1, LANES), f32),
        ),
        in_specs=[hbm] * len(operands),
        out_specs=(vmem,) * 4,
        scratch_shapes=[
            pltpu.VMEM((1, NB), jnp.int32),
            pltpu.VMEM((BLOCKS, BS, BS), bf16),
            pltpu.VMEM((BLOCKS, BS, BS), f32),
            pltpu.VMEM((CAP, BS, BS), bf16),
            pltpu.VMEM((CAP, BS, BS), bf16),
            pltpu.VMEM((CAP, BS, BS), f32),
            pltpu.VMEM((CAP, BS, BS), f32),
            pltpu.VMEM((N, BLOCKS, ROWS, LANES), bf16),
            pltpu.VMEM((NB + 1, ROWS, LANES), bf16),
            pltpu.VMEM((GROUPS, N, PER, ROWS, LANES), bf16),
            pltpu.VMEM((GROUPS, N, PER, ROWS, LANES), bf16),
            pltpu.VMEM((CAP, BS, BS), bf16),
            pltpu.VMEM((GROUPS, N, PER, ROWS, LANES), bf16),
            pltpu.VMEM((N * CAP, ROWS, LANES), bf16),
            pltpu.VMEM((N, BLOCKS, ROWS, LANES), bf16),
            pltpu.VMEM((N, 1, LANES), f32),
            pltpu.VMEM((LAYERS, 1, LANES), f32),
            pltpu.VMEM((1, N * CAP), jnp.int32),
            pltpu.VMEM((1, NB), jnp.int32),
            pltpu.SMEM((1, N * CAP), jnp.int32),
            pltpu.SMEM((1, NB), jnp.int32),
            pltpu.SemaphoreType.DMA((7,)),
            pltpu.SemaphoreType.DMA((2,)),
            pltpu.SemaphoreType.DMA((6,)),
            pltpu.SemaphoreType.DMA((GROUPS,)),
            pltpu.SemaphoreType.DMA((3,)),
            pltpu.SemaphoreType.DMA((2,)),
        ],
        compiler_params=pltpu.CompilerParams(
            collective_id=0, has_side_effects=True, vmem_limit_bytes=34 * MIB
        ),
        cost_estimate=pl.CostEstimate(
            flops=4 * 2 * CAP * BS**3, bytes_accessed=18 * MIB, transcendentals=0
        ),
        name="route_blocks",
    )(*operands)


def finish_kernel(left_ref, right_ref, home_ref, norms_ref,
                  update_ref, new_left_ref, new_right_ref, update, sems):
    outs = [
        pltpu.make_async_copy(left_ref, new_left_ref.at[0], sems.at[0]),
        pltpu.make_async_copy(right_ref, new_right_ref.at[0], sems.at[1]),
    ]
    for out in outs:
        out.start()
    entries = float(LAYERS * NB * BS * BS)
    clip_factor = jnp.minimum(1.0, UPDATE_RMS / jnp.sqrt(norms_ref[BLOCKS] / entries))
    for block in range(BLOCKS):
        pre = home_ref[:, block].astype(jnp.float32)
        pre_sq = jnp.full((1, LANES), jnp.sum(pre * pre), jnp.float32)
        ratio = jnp.sqrt(norms_ref[block] / float(BS * BS)) / jnp.sqrt(
            pre_sq / float(BS * BS) + NORM_FLOOR
        )
        factor = ratio * clip_factor
        for k in range(N):
            update[(block,) + piece_place(k)] = (pre[k] * factor).astype(jnp.bfloat16)
    out = pltpu.make_async_copy(update, update_ref.at[0], sems.at[2])
    out.start()
    for copy in outs + [out]:
        copy.wait()


def finish(new_left, new_right, home, norms):
    vmem = pl.BlockSpec(memory_space=pltpu.VMEM)
    hbm = pl.BlockSpec(memory_space=pltpu.HBM)
    return pl.pallas_call(
        finish_kernel,
        out_shape=(
            jax.ShapeDtypeStruct((1, BLOCKS, BS, BS), jnp.bfloat16),
            jax.ShapeDtypeStruct((1, CAP, BS, BS), jnp.float32),
            jax.ShapeDtypeStruct((1, CAP, BS, BS), jnp.float32),
        ),
        in_specs=[vmem] * 4,
        out_specs=(hbm,) * 3,
        scratch_shapes=[
            pltpu.VMEM((BLOCKS, BS, BS), jnp.bfloat16),
            pltpu.SemaphoreType.DMA((3,)),
        ],
        compiler_params=pltpu.CompilerParams(vmem_limit_bytes=8 * MIB),
        cost_estimate=pl.CostEstimate(
            flops=6 * BLOCKS * BS * BS, bytes_accessed=14 * MIB, transcendentals=0
        ),
        name="write_results",
    )(new_left, new_right, home, norms)


def per_device(gradients, second_moment, owners, left_stats, right_stats, left_root, right_root):
    owner_row = owners.reshape(1, NB)
    new_left, new_right, home, norms = routed(
        owner_row, gradients, second_moment, left_root, right_root, left_stats, right_stats
    )
    return finish(new_left, new_right, home, norms)


def solution(mesh):
    blocked = P("layer", "fsdp", None, None)
    return jax.shard_map(
        per_device,
        mesh=mesh,
        in_specs=(blocked, blocked, P("layer", None, None), blocked, blocked, blocked, blocked),
        out_specs=(blocked, blocked, blocked),
        check_vma=False,
    )
```

```python
import jax
import jax.numpy as jnp
from jax import lax
from jax.experimental import pallas as pl
from jax.experimental.pallas import tpu as pltpu
from jax.sharding import PartitionSpec as P

ADAM_EPS = 1e-08
DECAY_RATE = 0.95
UPDATE_RMS = 1.0
NORM_FLOOR = 1e-06

MESH = pl.DeviceIdType.MESH
RING = 4
CORES = 2
N = RING * RING * CORES
LAYERS = 4
BS = 256
BLOCKS = 8
NB = N * BLOCKS
CAP = 12
ROWS = 16
LANES = 128
GROUPS = 3
PER = CAP // GROUPS
MIB = 2**20


PLACES = (
    ((2, 2),),
    ((0, 2), (2, 0)),
    ((1, 2), (2, 3), (3, 2), (2, 1)),
    ((1, 1), (3, 3), (1, 3), (3, 1)),
    ((0, 1), (1, 0), (0, 3), (3, 0)),
)
STEPS = [
    (dz, dx, dc) for alike in PLACES for dc in range(CORES) for dz, dx in alike
] + [(0, 0, 1)]


def partner(me, step):
    dz, dx, dc = step
    z, x, c = me // (RING * CORES), (me // CORES) % RING, me % CORES
    return ((z + dz) % RING * RING + (x + dx) % RING) * CORES + (c + dc) % CORES


def by_core(me):
    z, x = me // (RING * CORES), (me // CORES) % RING
    places = [step[:2] for step in STEPS if step[2] == 0]

    def on_core(core):
        return [((z + dz) % RING * RING + (x + dx) % RING) * CORES + core for dz, dx in places]

    return on_core(0), on_core(1)


def piece_place(k):
    if isinstance(k, int):
        return pl.ds((k // 2) * ROWS, ROWS), pl.ds((k % 2) * LANES, LANES)
    rows = pl.ds(pl.multiple_of((k // 2) * ROWS, ROWS), ROWS)
    return rows, pl.ds(pl.multiple_of((k % 2) * LANES, LANES), LANES)


def join(pieces):
    return jnp.concatenate(
        [
            jnp.concatenate([pieces(2 * r + half) for r in range(BS // ROWS)], axis=0)
            for half in range(2)
        ],
        axis=1,
    )


def wait_bytes(ref, sem):
    pltpu.make_async_copy(ref, ref, sem).wait()


def slot_tables(owner_row):
    rows = lax.broadcasted_iota(jnp.int32, (NB, NB), 0)
    columns = lax.broadcasted_iota(jnp.int32, (NB, NB), 1)

    def upright(row):
        return jnp.sum(jnp.where(rows == columns, row, 0), axis=1, keepdims=True)

    same = (upright(owner_row) == owner_row) & (rows < columns)
    slot_index = owner_row * CAP + jnp.sum(jnp.where(same, 1, 0), axis=0, keepdims=True)
    slots = lax.broadcasted_iota(jnp.int32, (NB, N * CAP), 1)
    blocks = lax.broadcasted_iota(jnp.int32, (NB, N * CAP), 0)
    hit = upright(slot_index) == slots
    taken = NB + jnp.sum(jnp.where(hit, blocks - NB, 0), axis=0, keepdims=True)
    return taken, slot_index


def routed_kernel(
    owner_ref, grad_ref, second_ref, left_root_ref, right_root_ref, left_stats_ref, right_stats_ref,
    new_left_ref, new_right_ref, home_ref, norms_ref,
    owner_row, grad, second, left_root, right_root, left_stats, right_stats,
    leaving, spread, outgo, landed, owned, answer, arrived, homing, sums, totals,
    take_rows, back_rows, take_table, back_table,
    load_sems, table_sems, send_sems, route_sems, recv_sems, sum_sems,
):
    me = lax.axis_index("fsdp")
    layer = lax.axis_index("layer")

    loads = [
        pltpu.make_async_copy(src, dst, load_sems.at[index])
        for index, (src, dst) in enumerate(
            (
                (grad_ref.at[0], grad),
                (owner_ref, owner_row),
                (second_ref.at[0], second),
                (left_root_ref.at[0], left_root),
                (right_root_ref.at[0], right_root),
                (left_stats_ref.at[0], left_stats),
                (right_stats_ref.at[0], right_stats),
            )
        )
    ]
    loads[0].start()
    loads[1].start()
    barrier = pltpu.get_barrier_semaphore()
    for step in STEPS:
        pl.semaphore_signal(
            barrier, inc=1, device_id={"fsdp": partner(me, step)}, device_id_type=MESH
        )
    for offset in range(1, LAYERS):
        pl.semaphore_signal(
            barrier,
            inc=1,
            device_id={"layer": (layer + offset) % LAYERS},
            device_id_type=MESH,
        )
    loads[0].wait()
    pl.semaphore_wait(barrier, N - 1 + LAYERS - 1)

    def remote(src, dst, send_sem, recv_sem, target):
        copy = pltpu.make_async_remote_copy(
            src_ref=src,
            dst_ref=dst,
            send_sem=send_sem,
            recv_sem=recv_sem,
            device_id={"fsdp": target},
            device_id_type=MESH,
        )
        copy.start()

    targets = [partner(me, step) for step in STEPS]
    my_blocks = pl.ds(me * BLOCKS, BLOCKS)

    to_core = by_core(me)
    sibling = partner(me, (0, 0, 1))
    for target in to_core[0] + [sibling] + to_core[1]:
        leaving[target] = grad[(slice(None),) + piece_place(target)]
        remote(
            leaving.at[target], spread.at[my_blocks], send_sems.at[0], recv_sems.at[0], target
        )
    spread[my_blocks] = grad[(slice(None),) + piece_place(me)]
    spread[NB] = jnp.zeros((ROWS, LANES), jnp.bfloat16)

    for load in loads[2:]:
        load.start()
    loads[1].wait()
    take_rows[...], back_rows[...] = slot_tables(owner_row[...])
    tables = [
        pltpu.make_async_copy(take_rows, take_table, table_sems.at[0]),
        pltpu.make_async_copy(back_rows, back_table, table_sems.at[1]),
    ]
    for table in tables:
        table.start()
    loads[2].wait()

    def adam_block(b, total):
        row_sum = jnp.zeros((8, LANES), jnp.float32)
        for half in range(2):
            for quarter in range(4):
                rows = pl.ds(quarter * 64, 64)
                lanes = pl.ds(half * LANES, LANES)
                direction = grad[b, rows, lanes].astype(jnp.float32) / (
                    jnp.sqrt(second[b, rows, lanes]) + ADAM_EPS
                )
                row_sum += jnp.sum((direction * direction).reshape(8, 8, LANES), axis=0)
        block_sum = jnp.full((1, LANES), jnp.sum(row_sum), jnp.float32)
        norms_ref[b] = block_sum
        return total + block_sum

    sums[N - 1] = lax.fori_loop(0, BLOCKS, adam_block, jnp.zeros((1, LANES), jnp.float32))

    for table in tables:
        table.wait()
    wait_bytes(spread.at[pl.ds(0, NB - BLOCKS)], recv_sems.at[0])

    def take(ref, group, target):
        for slot in range(PER):
            ref[group, target, slot] = spread[take_table[0, target * CAP + group * PER + slot]]

    for group in range(GROUPS):
        for target in targets:
            take(outgo, group, target)
            remote(
                outgo.at[group, target],
                landed.at[group, me],
                send_sems.at[1],
                route_sems.at[group],
                target,
            )
        take(landed, group, me)

    for index, target in enumerate(targets):
        remote(sums.at[N - 1], sums.at[index], send_sems.at[4], sum_sems.at[0], target)

    loads[3].wait()
    loads[4].wait()
    def send_answers(group, core):
        landing = pl.ds(me * CAP + group * PER, PER)
        for target in to_core[core] + ([sibling] if core == 0 else []):
            remote(
                answer.at[group, target],
                arrived.at[landing],
                send_sems.at[2],
                recv_sems.at[1],
                target,
            )
        if core == 0:
            arrived[landing] = answer[group, me]

    for group in range(GROUPS):
        wait_bytes(landed.at[group, pl.ds(0, N - 1)], route_sems.at[group])
        if group > 0:
            send_answers(group - 1, 0)

        def precondition(index, carry):
            slot = group * PER + index
            block = join(lambda k: landed[group, k, index])
            owned[slot] = block
            half_done = jnp.dot(
                left_root[slot], block, preferred_element_type=jnp.float32
            ).astype(jnp.bfloat16)
            full = jnp.dot(
                half_done, right_root[slot], preferred_element_type=jnp.float32
            ).astype(jnp.bfloat16)
            for k in range(N):
                r, half = divmod(k, 2)
                answer[group, k, index] = full[
                    r * ROWS : (r + 1) * ROWS, half * LANES : (half + 1) * LANES
                ]
            return carry

        lax.fori_loop(0, PER, precondition, 0)

    send_answers(GROUPS - 1, 0)
    for group in range(GROUPS):
        send_answers(group, 1)

    wait_bytes(sums.at[pl.ds(0, N - 1)], sum_sems.at[0])
    totals[LAYERS - 1] = jnp.sum(sums[...], axis=0)
    for offset in range(1, LAYERS):
        pltpu.make_async_remote_copy(
            src_ref=totals.at[LAYERS - 1],
            dst_ref=totals.at[offset - 1],
            send_sem=send_sems.at[5],
            recv_sem=sum_sems.at[1],
            device_id={"layer": (layer + offset) % LAYERS},
            device_id_type=MESH,
        ).start()

    wait_bytes(arrived.at[pl.ds(0, CAP * (N - 1))], recv_sems.at[1])

    def give(ref, target):
        for block in range(BLOCKS):
            ref[target, block] = arrived[back_table[0, target * BLOCKS + block]]

    for target in targets:
        give(homing, target)
        remote(homing.at[target], home_ref.at[me], send_sems.at[3], recv_sems.at[2], target)
    give(home_ref, me)

    loads[5].wait()
    loads[6].wait()

    def statistics(slot, carry):
        block = owned[slot]
        gram_left = lax.dot_general(
            block, block, (((1,), (1,)), ((), ())), preferred_element_type=jnp.float32
        )
        gram_right = lax.dot_general(
            block, block, (((0,), (0,)), ((), ())), preferred_element_type=jnp.float32
        )
        new_left_ref[slot] = DECAY_RATE * left_stats[slot] + (1.0 - DECAY_RATE) * gram_left
        new_right_ref[slot] = DECAY_RATE * right_stats[slot] + (1.0 - DECAY_RATE) * gram_right
        return carry

    lax.fori_loop(0, CAP, statistics, 0)


    wait_bytes(totals.at[pl.ds(0, LAYERS - 1)], sum_sems.at[1])
    norms_ref[BLOCKS] = jnp.sum(totals[...], axis=0)
    wait_bytes(leaving.at[pl.ds(0, N - 1)], send_sems.at[0])
    wait_bytes(arrived.at[pl.ds(0, CAP * (N - 1))], send_sems.at[1])
    wait_bytes(arrived.at[pl.ds(0, CAP * (N - 1))], send_sems.at[2])
    wait_bytes(sums.at[pl.ds(0, N - 1)], send_sems.at[4])
    wait_bytes(totals.at[pl.ds(0, LAYERS - 1)], send_sems.at[5])
    wait_bytes(homing.at[pl.ds(0, N - 1)], send_sems.at[3])
    wait_bytes(home_ref.at[pl.ds(0, N - 1)], recv_sems.at[2])


def routed(owner_row, gradients, second_moment, left_root, right_root, left_stats, right_stats):
    bf16, f32 = jnp.bfloat16, jnp.float32
    vmem = pl.BlockSpec(memory_space=pltpu.VMEM)
    hbm = pl.BlockSpec(memory_space=pltpu.HBM)
    operands = [
        pltpu.with_memory_space_constraint(array, pltpu.HBM)
        for array in (
            owner_row, gradients, second_moment, left_root, right_root, left_stats, right_stats
        )
    ]
    return pl.pallas_call(
        routed_kernel,
        out_shape=(
            pltpu.VMEM((CAP, BS, BS), f32),
            pltpu.VMEM((CAP, BS, BS), f32),
            pltpu.VMEM((N, BLOCKS, ROWS, LANES), bf16),
            pltpu.VMEM((BLOCKS + 1, 1, LANES), f32),
        ),
        in_specs=[hbm] * len(operands),
        out_specs=(vmem,) * 4,
        scratch_shapes=[
            pltpu.VMEM((1, NB), jnp.int32),
            pltpu.VMEM((BLOCKS, BS, BS), bf16),
            pltpu.VMEM((BLOCKS, BS, BS), f32),
            pltpu.VMEM((CAP, BS, BS), bf16),
            pltpu.VMEM((CAP, BS, BS), bf16),
            pltpu.VMEM((CAP, BS, BS), f32),
            pltpu.VMEM((CAP, BS, BS), f32),
            pltpu.VMEM((N, BLOCKS, ROWS, LANES), bf16),
            pltpu.VMEM((NB + 1, ROWS, LANES), bf16),
            pltpu.VMEM((GROUPS, N, PER, ROWS, LANES), bf16),
            pltpu.VMEM((GROUPS, N, PER, ROWS, LANES), bf16),
            pltpu.VMEM((CAP, BS, BS), bf16),
            pltpu.VMEM((GROUPS, N, PER, ROWS, LANES), bf16),
            pltpu.VMEM((N * CAP, ROWS, LANES), bf16),
            pltpu.VMEM((N, BLOCKS, ROWS, LANES), bf16),
            pltpu.VMEM((N, 1, LANES), f32),
            pltpu.VMEM((LAYERS, 1, LANES), f32),
            pltpu.VMEM((1, N * CAP), jnp.int32),
            pltpu.VMEM((1, NB), jnp.int32),
            pltpu.SMEM((1, N * CAP), jnp.int32),
            pltpu.SMEM((1, NB), jnp.int32),
            pltpu.SemaphoreType.DMA((7,)),
            pltpu.SemaphoreType.DMA((2,)),
            pltpu.SemaphoreType.DMA((6,)),
            pltpu.SemaphoreType.DMA((GROUPS,)),
            pltpu.SemaphoreType.DMA((3,)),
            pltpu.SemaphoreType.DMA((2,)),
        ],
        compiler_params=pltpu.CompilerParams(
            collective_id=0, has_side_effects=True, vmem_limit_bytes=34 * MIB
        ),
        cost_estimate=pl.CostEstimate(
            flops=4 * 2 * CAP * BS**3, bytes_accessed=18 * MIB, transcendentals=0
        ),
        name="route_blocks",
    )(*operands)


def finish_kernel(left_ref, right_ref, home_ref, norms_ref,
                  update_ref, new_left_ref, new_right_ref, update, sems):
    outs = [
        pltpu.make_async_copy(left_ref, new_left_ref.at[0], sems.at[0]),
        pltpu.make_async_copy(right_ref, new_right_ref.at[0], sems.at[1]),
    ]
    for out in outs:
        out.start()
    entries = float(LAYERS * NB * BS * BS)
    clip_factor = jnp.minimum(1.0, UPDATE_RMS / jnp.sqrt(norms_ref[BLOCKS] / entries))
    for block in range(BLOCKS):
        pre = home_ref[:, block].astype(jnp.float32)
        pre_sq = jnp.full((1, LANES), jnp.sum(pre * pre), jnp.float32)
        ratio = jnp.sqrt(norms_ref[block] / float(BS * BS)) / jnp.sqrt(
            pre_sq / float(BS * BS) + NORM_FLOOR
        )
        factor = ratio * clip_factor
        for k in range(N):
            update[(block,) + piece_place(k)] = (pre[k] * factor).astype(jnp.bfloat16)
    out = pltpu.make_async_copy(update, update_ref.at[0], sems.at[2])
    out.start()
    for copy in outs + [out]:
        copy.wait()


def finish(new_left, new_right, home, norms):
    vmem = pl.BlockSpec(memory_space=pltpu.VMEM)
    hbm = pl.BlockSpec(memory_space=pltpu.HBM)
    return pl.pallas_call(
        finish_kernel,
        out_shape=(
            jax.ShapeDtypeStruct((1, BLOCKS, BS, BS), jnp.bfloat16),
            jax.ShapeDtypeStruct((1, CAP, BS, BS), jnp.float32),
            jax.ShapeDtypeStruct((1, CAP, BS, BS), jnp.float32),
        ),
        in_specs=[vmem] * 4,
        out_specs=(hbm,) * 3,
        scratch_shapes=[
            pltpu.VMEM((BLOCKS, BS, BS), jnp.bfloat16),
            pltpu.SemaphoreType.DMA((3,)),
        ],
        compiler_params=pltpu.CompilerParams(vmem_limit_bytes=8 * MIB),
        cost_estimate=pl.CostEstimate(
            flops=6 * BLOCKS * BS * BS, bytes_accessed=14 * MIB, transcendentals=0
        ),
        name="write_results",
    )(new_left, new_right, home, norms)


def per_device(gradients, second_moment, owners, left_stats, right_stats, left_root, right_root):
    owner_row = owners.reshape(1, NB)
    new_left, new_right, home, norms = routed(
        owner_row, gradients, second_moment, left_root, right_root, left_stats, right_stats
    )
    return finish(new_left, new_right, home, norms)


def solution(mesh):
    blocked = P("layer", "fsdp", None, None)
    return jax.shard_map(
        per_device,
        mesh=mesh,
        in_specs=(blocked, blocked, P("layer", None, None), blocked, blocked, blocked, blocked),
        out_specs=(blocked, blocked, blocked),
        check_vma=False,
    )
```

```python
import jax
import jax.numpy as jnp
from jax import lax
from jax.experimental import pallas as pl
from jax.experimental.pallas import tpu as pltpu
from jax.sharding import PartitionSpec as P

ADAM_EPS = 1e-08
DECAY_RATE = 0.95
UPDATE_RMS = 1.0
NORM_FLOOR = 1e-06

MESH = pl.DeviceIdType.MESH
RING = 4
CORES = 2
N = RING * RING * CORES
LAYERS = 4
BS = 256
BLOCKS = 8
NB = N * BLOCKS
CAP = 12
ROWS = 16
LANES = 128
GROUPS = 3
PER = CAP // GROUPS
MIB = 2**20


PLACES = (
    ((2, 2),),
    ((0, 2), (2, 0)),
    ((1, 1), (3, 3), (1, 3), (3, 1)),
    ((1, 2), (2, 3), (3, 2), (2, 1)),
    ((0, 1), (1, 0), (0, 3), (3, 0)),
)
STEPS = [
    (dz, dx, dc) for alike in PLACES for dc in range(CORES) for dz, dx in alike
] + [(0, 0, 1)]


def partner(me, step):
    dz, dx, dc = step
    z, x, c = me // (RING * CORES), (me // CORES) % RING, me % CORES
    return ((z + dz) % RING * RING + (x + dx) % RING) * CORES + (c + dc) % CORES


def by_core(me):
    z, x = me // (RING * CORES), (me // CORES) % RING
    places = [step[:2] for step in STEPS if step[2] == 0]

    def on_core(core):
        return [((z + dz) % RING * RING + (x + dx) % RING) * CORES + core for dz, dx in places]

    return on_core(0), on_core(1)


def piece_place(k):
    if isinstance(k, int):
        return pl.ds((k // 2) * ROWS, ROWS), pl.ds((k % 2) * LANES, LANES)
    rows = pl.ds(pl.multiple_of((k // 2) * ROWS, ROWS), ROWS)
    return rows, pl.ds(pl.multiple_of((k % 2) * LANES, LANES), LANES)


def join(pieces):
    return jnp.concatenate(
        [
            jnp.concatenate([pieces(2 * r + half) for r in range(BS // ROWS)], axis=0)
            for half in range(2)
        ],
        axis=1,
    )


def wait_bytes(ref, sem):
    pltpu.make_async_copy(ref, ref, sem).wait()


def slot_tables(owner_row):
    rows = lax.broadcasted_iota(jnp.int32, (NB, NB), 0)
    columns = lax.broadcasted_iota(jnp.int32, (NB, NB), 1)

    def upright(row):
        return jnp.sum(jnp.where(rows == columns, row, 0), axis=1, keepdims=True)

    same = (upright(owner_row) == owner_row) & (rows < columns)
    slot_index = owner_row * CAP + jnp.sum(jnp.where(same, 1, 0), axis=0, keepdims=True)
    slots = lax.broadcasted_iota(jnp.int32, (NB, N * CAP), 1)
    blocks = lax.broadcasted_iota(jnp.int32, (NB, N * CAP), 0)
    hit = upright(slot_index) == slots
    taken = NB + jnp.sum(jnp.where(hit, blocks - NB, 0), axis=0, keepdims=True)
    return taken, slot_index


def routed_kernel(
    owner_ref, grad_ref, second_ref, left_root_ref, right_root_ref, left_stats_ref, right_stats_ref,
    new_left_ref, new_right_ref, home_ref, norms_ref,
    owner_row, grad, second, left_root, right_root, left_stats, right_stats,
    leaving, spread, outgo, landed, owned, answer, arrived, homing, sums, totals,
    take_rows, back_rows, take_table, back_table,
    load_sems, table_sems, send_sems, route_sems, recv_sems, sum_sems,
):
    me = lax.axis_index("fsdp")
    layer = lax.axis_index("layer")

    loads = [
        pltpu.make_async_copy(src, dst, load_sems.at[index])
        for index, (src, dst) in enumerate(
            (
                (grad_ref.at[0], grad),
                (owner_ref, owner_row),
                (second_ref.at[0], second),
                (left_root_ref.at[0], left_root),
                (right_root_ref.at[0], right_root),
                (left_stats_ref.at[0], left_stats),
                (right_stats_ref.at[0], right_stats),
            )
        )
    ]
    loads[0].start()
    loads[1].start()
    barrier = pltpu.get_barrier_semaphore()
    for step in STEPS:
        pl.semaphore_signal(
            barrier, inc=1, device_id={"fsdp": partner(me, step)}, device_id_type=MESH
        )
    for offset in range(1, LAYERS):
        pl.semaphore_signal(
            barrier,
            inc=1,
            device_id={"layer": (layer + offset) % LAYERS},
            device_id_type=MESH,
        )
    loads[0].wait()
    pl.semaphore_wait(barrier, N - 1 + LAYERS - 1)

    def remote(src, dst, send_sem, recv_sem, target):
        copy = pltpu.make_async_remote_copy(
            src_ref=src,
            dst_ref=dst,
            send_sem=send_sem,
            recv_sem=recv_sem,
            device_id={"fsdp": target},
            device_id_type=MESH,
        )
        copy.start()

    targets = [partner(me, step) for step in STEPS]
    my_blocks = pl.ds(me * BLOCKS, BLOCKS)

    to_core = by_core(me)
    sibling = partner(me, (0, 0, 1))
    for target in to_core[0] + [sibling] + to_core[1]:
        leaving[target] = grad[(slice(None),) + piece_place(target)]
        remote(
            leaving.at[target], spread.at[my_blocks], send_sems.at[0], recv_sems.at[0], target
        )
    spread[my_blocks] = grad[(slice(None),) + piece_place(me)]
    spread[NB] = jnp.zeros((ROWS, LANES), jnp.bfloat16)

    for load in loads[2:]:
        load.start()
    loads[1].wait()
    take_rows[...], back_rows[...] = slot_tables(owner_row[...])
    tables = [
        pltpu.make_async_copy(take_rows, take_table, table_sems.at[0]),
        pltpu.make_async_copy(back_rows, back_table, table_sems.at[1]),
    ]
    for table in tables:
        table.start()
    loads[2].wait()

    def adam_block(b, total):
        row_sum = jnp.zeros((8, LANES), jnp.float32)
        for half in range(2):
            for quarter in range(4):
                rows = pl.ds(quarter * 64, 64)
                lanes = pl.ds(half * LANES, LANES)
                direction = grad[b, rows, lanes].astype(jnp.float32) / (
                    jnp.sqrt(second[b, rows, lanes]) + ADAM_EPS
                )
                row_sum += jnp.sum((direction * direction).reshape(8, 8, LANES), axis=0)
        block_sum = jnp.full((1, LANES), jnp.sum(row_sum), jnp.float32)
        norms_ref[b] = block_sum
        return total + block_sum

    sums[N - 1] = lax.fori_loop(0, BLOCKS, adam_block, jnp.zeros((1, LANES), jnp.float32))

    for table in tables:
        table.wait()
    wait_bytes(spread.at[pl.ds(0, NB - BLOCKS)], recv_sems.at[0])

    def take(ref, group, target):
        for slot in range(PER):
            ref[group, target, slot] = spread[take_table[0, target * CAP + group * PER + slot]]

    for group in range(GROUPS):
        for target in targets:
            take(outgo, group, target)
            remote(
                outgo.at[group, target],
                landed.at[group, me],
                send_sems.at[1],
                route_sems.at[group],
                target,
            )
        take(landed, group, me)

    for index, target in enumerate(targets):
        remote(sums.at[N - 1], sums.at[index], send_sems.at[4], sum_sems.at[0], target)

    loads[3].wait()
    loads[4].wait()
    def send_answers(group, core):
        landing = pl.ds(me * CAP + group * PER, PER)
        for target in to_core[core] + ([sibling] if core == 0 else []):
            remote(
                answer.at[group, target],
                arrived.at[landing],
                send_sems.at[2],
                recv_sems.at[1],
                target,
            )
        if core == 0:
            arrived[landing] = answer[group, me]

    for group in range(GROUPS):
        wait_bytes(landed.at[group, pl.ds(0, N - 1)], route_sems.at[group])
        if group > 0:
            send_answers(group - 1, 0)

        def precondition(index, carry):
            slot = group * PER + index
            block = join(lambda k: landed[group, k, index])
            owned[slot] = block
            half_done = jnp.dot(
                left_root[slot], block, preferred_element_type=jnp.float32
            ).astype(jnp.bfloat16)
            full = jnp.dot(
                half_done, right_root[slot], preferred_element_type=jnp.float32
            ).astype(jnp.bfloat16)
            for k in range(N):
                r, half = divmod(k, 2)
                answer[group, k, index] = full[
                    r * ROWS : (r + 1) * ROWS, half * LANES : (half + 1) * LANES
                ]
            return carry

        lax.fori_loop(0, PER, precondition, 0)

    send_answers(GROUPS - 1, 0)
    for group in range(GROUPS):
        send_answers(group, 1)

    wait_bytes(sums.at[pl.ds(0, N - 1)], sum_sems.at[0])
    totals[LAYERS - 1] = jnp.sum(sums[...], axis=0)
    for offset in range(1, LAYERS):
        pltpu.make_async_remote_copy(
            src_ref=totals.at[LAYERS - 1],
            dst_ref=totals.at[offset - 1],
            send_sem=send_sems.at[5],
            recv_sem=sum_sems.at[1],
            device_id={"layer": (layer + offset) % LAYERS},
            device_id_type=MESH,
        ).start()

    wait_bytes(arrived.at[pl.ds(0, CAP * (N - 1))], recv_sems.at[1])

    def give(ref, target):
        for block in range(BLOCKS):
            ref[target, block] = arrived[back_table[0, target * BLOCKS + block]]

    for target in targets:
        give(homing, target)
        remote(homing.at[target], home_ref.at[me], send_sems.at[3], recv_sems.at[2], target)
    give(home_ref, me)

    loads[5].wait()
    loads[6].wait()

    def statistics(slot, carry):
        block = owned[slot]
        gram_left = lax.dot_general(
            block, block, (((1,), (1,)), ((), ())), preferred_element_type=jnp.float32
        )
        gram_right = lax.dot_general(
            block, block, (((0,), (0,)), ((), ())), preferred_element_type=jnp.float32
        )
        new_left_ref[slot] = DECAY_RATE * left_stats[slot] + (1.0 - DECAY_RATE) * gram_left
        new_right_ref[slot] = DECAY_RATE * right_stats[slot] + (1.0 - DECAY_RATE) * gram_right
        return carry

    lax.fori_loop(0, CAP, statistics, 0)


    wait_bytes(totals.at[pl.ds(0, LAYERS - 1)], sum_sems.at[1])
    norms_ref[BLOCKS] = jnp.sum(totals[...], axis=0)
    wait_bytes(leaving.at[pl.ds(0, N - 1)], send_sems.at[0])
    wait_bytes(arrived.at[pl.ds(0, CAP * (N - 1))], send_sems.at[1])
    wait_bytes(arrived.at[pl.ds(0, CAP * (N - 1))], send_sems.at[2])
    wait_bytes(sums.at[pl.ds(0, N - 1)], send_sems.at[4])
    wait_bytes(totals.at[pl.ds(0, LAYERS - 1)], send_sems.at[5])
    wait_bytes(homing.at[pl.ds(0, N - 1)], send_sems.at[3])
    wait_bytes(home_ref.at[pl.ds(0, N - 1)], recv_sems.at[2])


def routed(owner_row, gradients, second_moment, left_root, right_root, left_stats, right_stats):
    bf16, f32 = jnp.bfloat16, jnp.float32
    vmem = pl.BlockSpec(memory_space=pltpu.VMEM)
    hbm = pl.BlockSpec(memory_space=pltpu.HBM)
    operands = [
        pltpu.with_memory_space_constraint(array, pltpu.HBM)
        for array in (
            owner_row, gradients, second_moment, left_root, right_root, left_stats, right_stats
        )
    ]
    return pl.pallas_call(
        routed_kernel,
        out_shape=(
            pltpu.VMEM((CAP, BS, BS), f32),
            pltpu.VMEM((CAP, BS, BS), f32),
            pltpu.VMEM((N, BLOCKS, ROWS, LANES), bf16),
            pltpu.VMEM((BLOCKS + 1, 1, LANES), f32),
        ),
        in_specs=[hbm] * len(operands),
        out_specs=(vmem,) * 4,
        scratch_shapes=[
            pltpu.VMEM((1, NB), jnp.int32),
            pltpu.VMEM((BLOCKS, BS, BS), bf16),
            pltpu.VMEM((BLOCKS, BS, BS), f32),
            pltpu.VMEM((CAP, BS, BS), bf16),
            pltpu.VMEM((CAP, BS, BS), bf16),
            pltpu.VMEM((CAP, BS, BS), f32),
            pltpu.VMEM((CAP, BS, BS), f32),
            pltpu.VMEM((N, BLOCKS, ROWS, LANES), bf16),
            pltpu.VMEM((NB + 1, ROWS, LANES), bf16),
            pltpu.VMEM((GROUPS, N, PER, ROWS, LANES), bf16),
            pltpu.VMEM((GROUPS, N, PER, ROWS, LANES), bf16),
            pltpu.VMEM((CAP, BS, BS), bf16),
            pltpu.VMEM((GROUPS, N, PER, ROWS, LANES), bf16),
            pltpu.VMEM((N * CAP, ROWS, LANES), bf16),
            pltpu.VMEM((N, BLOCKS, ROWS, LANES), bf16),
            pltpu.VMEM((N, 1, LANES), f32),
            pltpu.VMEM((LAYERS, 1, LANES), f32),
            pltpu.VMEM((1, N * CAP), jnp.int32),
            pltpu.VMEM((1, NB), jnp.int32),
            pltpu.SMEM((1, N * CAP), jnp.int32),
            pltpu.SMEM((1, NB), jnp.int32),
            pltpu.SemaphoreType.DMA((7,)),
            pltpu.SemaphoreType.DMA((2,)),
            pltpu.SemaphoreType.DMA((6,)),
            pltpu.SemaphoreType.DMA((GROUPS,)),
            pltpu.SemaphoreType.DMA((3,)),
            pltpu.SemaphoreType.DMA((2,)),
        ],
        compiler_params=pltpu.CompilerParams(
            collective_id=0, has_side_effects=True, vmem_limit_bytes=34 * MIB
        ),
        cost_estimate=pl.CostEstimate(
            flops=4 * 2 * CAP * BS**3, bytes_accessed=18 * MIB, transcendentals=0
        ),
        name="route_blocks",
    )(*operands)


def finish_kernel(left_ref, right_ref, home_ref, norms_ref,
                  update_ref, new_left_ref, new_right_ref, update, sems):
    outs = [
        pltpu.make_async_copy(left_ref, new_left_ref.at[0], sems.at[0]),
        pltpu.make_async_copy(right_ref, new_right_ref.at[0], sems.at[1]),
    ]
    for out in outs:
        out.start()
    entries = float(LAYERS * NB * BS * BS)
    clip_factor = jnp.minimum(1.0, UPDATE_RMS / jnp.sqrt(norms_ref[BLOCKS] / entries))
    for block in range(BLOCKS):
        pre = home_ref[:, block].astype(jnp.float32)
        pre_sq = jnp.full((1, LANES), jnp.sum(pre * pre), jnp.float32)
        ratio = jnp.sqrt(norms_ref[block] / float(BS * BS)) / jnp.sqrt(
            pre_sq / float(BS * BS) + NORM_FLOOR
        )
        factor = ratio * clip_factor
        for k in range(N):
            update[(block,) + piece_place(k)] = (pre[k] * factor).astype(jnp.bfloat16)
    out = pltpu.make_async_copy(update, update_ref.at[0], sems.at[2])
    out.start()
    for copy in outs + [out]:
        copy.wait()


def finish(new_left, new_right, home, norms):
    vmem = pl.BlockSpec(memory_space=pltpu.VMEM)
    hbm = pl.BlockSpec(memory_space=pltpu.HBM)
    return pl.pallas_call(
        finish_kernel,
        out_shape=(
            jax.ShapeDtypeStruct((1, BLOCKS, BS, BS), jnp.bfloat16),
            jax.ShapeDtypeStruct((1, CAP, BS, BS), jnp.float32),
            jax.ShapeDtypeStruct((1, CAP, BS, BS), jnp.float32),
        ),
        in_specs=[vmem] * 4,
        out_specs=(hbm,) * 3,
        scratch_shapes=[
            pltpu.VMEM((BLOCKS, BS, BS), jnp.bfloat16),
            pltpu.SemaphoreType.DMA((3,)),
        ],
        compiler_params=pltpu.CompilerParams(vmem_limit_bytes=8 * MIB),
        cost_estimate=pl.CostEstimate(
            flops=6 * BLOCKS * BS * BS, bytes_accessed=14 * MIB, transcendentals=0
        ),
        name="write_results",
    )(new_left, new_right, home, norms)


def per_device(gradients, second_moment, owners, left_stats, right_stats, left_root, right_root):
    owner_row = owners.reshape(1, NB)
    new_left, new_right, home, norms = routed(
        owner_row, gradients, second_moment, left_root, right_root, left_stats, right_stats
    )
    return finish(new_left, new_right, home, norms)


def solution(mesh):
    blocked = P("layer", "fsdp", None, None)
    return jax.shard_map(
        per_device,
        mesh=mesh,
        in_specs=(blocked, blocked, P("layer", None, None), blocked, blocked, blocked, blocked),
        out_specs=(blocked, blocked, blocked),
        check_vma=False,
    )
```

```python
import jax
import jax.numpy as jnp
from jax import lax
from jax.experimental import pallas as pl
from jax.experimental.pallas import tpu as pltpu
from jax.sharding import PartitionSpec as P

ADAM_EPS = 1e-08
DECAY_RATE = 0.95
UPDATE_RMS = 1.0
NORM_FLOOR = 1e-06

MESH = pl.DeviceIdType.MESH
RING = 4
CORES = 2
N = RING * RING * CORES
LAYERS = 4
BS = 256
BLOCKS = 8
NB = N * BLOCKS
CAP = 12
ROWS = 16
LANES = 128
GROUPS = 3
PER = CAP // GROUPS
MIB = 2**20


PLACES = (
    ((2, 2),),
    ((0, 2), (2, 0)),
    ((1, 1), (3, 3), (1, 3), (3, 1)),
    ((1, 2), (2, 3), (3, 2), (2, 1)),
    ((0, 1), (1, 0), (0, 3), (3, 0)),
)
STEPS = [
    (dz, dx, dc) for alike in PLACES for dc in range(CORES) for dz, dx in alike
] + [(0, 0, 1)]


def partner(me, step):
    dz, dx, dc = step
    z, x, c = me // (RING * CORES), (me // CORES) % RING, me % CORES
    return ((z + dz) % RING * RING + (x + dx) % RING) * CORES + (c + dc) % CORES


def by_core(me):
    z, x = me // (RING * CORES), (me // CORES) % RING
    places = [step[:2] for step in STEPS if step[2] == 0]

    def on_core(core):
        return [((z + dz) % RING * RING + (x + dx) % RING) * CORES + core for dz, dx in places]

    return on_core(0), on_core(1)


def piece_place(k):
    if isinstance(k, int):
        return pl.ds((k // 2) * ROWS, ROWS), pl.ds((k % 2) * LANES, LANES)
    rows = pl.ds(pl.multiple_of((k // 2) * ROWS, ROWS), ROWS)
    return rows, pl.ds(pl.multiple_of((k % 2) * LANES, LANES), LANES)


def join(pieces):
    return jnp.concatenate(
        [
            jnp.concatenate([pieces(2 * r + half) for r in range(BS // ROWS)], axis=0)
            for half in range(2)
        ],
        axis=1,
    )


def wait_bytes(ref, sem):
    pltpu.make_async_copy(ref, ref, sem).wait()


def slot_tables(owner_row):
    rows = lax.broadcasted_iota(jnp.int32, (NB, NB), 0)
    columns = lax.broadcasted_iota(jnp.int32, (NB, NB), 1)

    def upright(row):
        return jnp.sum(jnp.where(rows == columns, row, 0), axis=1, keepdims=True)

    same = (upright(owner_row) == owner_row) & (rows < columns)
    slot_index = owner_row * CAP + jnp.sum(jnp.where(same, 1, 0), axis=0, keepdims=True)
    slots = lax.broadcasted_iota(jnp.int32, (NB, N * CAP), 1)
    blocks = lax.broadcasted_iota(jnp.int32, (NB, N * CAP), 0)
    hit = upright(slot_index) == slots
    taken = NB + jnp.sum(jnp.where(hit, blocks - NB, 0), axis=0, keepdims=True)
    return taken, slot_index


def routed_kernel(
    owner_ref, grad_ref, second_ref, left_root_ref, right_root_ref, left_stats_ref, right_stats_ref,
    new_left_ref, new_right_ref, home_ref, norms_ref,
    owner_row, grad, second, left_root, right_root, left_stats, right_stats,
    leaving, spread, outgo, landed, owned, answer, arrived, homing, sums, totals,
    take_rows, back_rows, take_table, back_table,
    load_sems, table_sems, send_sems, route_sems, recv_sems, sum_sems,
):
    me = lax.axis_index("fsdp")
    layer = lax.axis_index("layer")

    loads = [
        pltpu.make_async_copy(src, dst, load_sems.at[index])
        for index, (src, dst) in enumerate(
            (
                (grad_ref.at[0], grad),
                (owner_ref, owner_row),
                (second_ref.at[0], second),
                (left_root_ref.at[0], left_root),
                (right_root_ref.at[0], right_root),
                (left_stats_ref.at[0], left_stats),
                (right_stats_ref.at[0], right_stats),
            )
        )
    ]
    loads[0].start()
    loads[1].start()
    barrier = pltpu.get_barrier_semaphore()
    for step in STEPS:
        pl.semaphore_signal(
            barrier, inc=1, device_id={"fsdp": partner(me, step)}, device_id_type=MESH
        )
    for offset in range(1, LAYERS):
        pl.semaphore_signal(
            barrier,
            inc=1,
            device_id={"layer": (layer + offset) % LAYERS},
            device_id_type=MESH,
        )
    loads[0].wait()
    pl.semaphore_wait(barrier, N - 1 + LAYERS - 1)

    def remote(src, dst, send_sem, recv_sem, target):
        copy = pltpu.make_async_remote_copy(
            src_ref=src,
            dst_ref=dst,
            send_sem=send_sem,
            recv_sem=recv_sem,
            device_id={"fsdp": target},
            device_id_type=MESH,
        )
        copy.start()

    targets = [partner(me, step) for step in STEPS]
    my_blocks = pl.ds(me * BLOCKS, BLOCKS)

    to_core = by_core(me)
    sibling = partner(me, (0, 0, 1))
    for target in to_core[0] + [sibling] + to_core[1]:
        leaving[target] = grad[(slice(None),) + piece_place(target)]
        remote(
            leaving.at[target], spread.at[my_blocks], send_sems.at[0], recv_sems.at[0], target
        )
    spread[my_blocks] = grad[(slice(None),) + piece_place(me)]
    spread[NB] = jnp.zeros((ROWS, LANES), jnp.bfloat16)

    for load in loads[2:]:
        load.start()
    loads[1].wait()
    take_rows[...], back_rows[...] = slot_tables(owner_row[...])
    tables = [
        pltpu.make_async_copy(take_rows, take_table, table_sems.at[0]),
        pltpu.make_async_copy(back_rows, back_table, table_sems.at[1]),
    ]
    for table in tables:
        table.start()
    for table in tables:
        table.wait()
    wait_bytes(spread.at[pl.ds(0, NB - BLOCKS)], recv_sems.at[0])

    def take(ref, group, target):
        for slot in range(PER):
            ref[group, target, slot] = spread[take_table[0, target * CAP + group * PER + slot]]

    for group in range(GROUPS):
        for target in targets:
            take(outgo, group, target)
            remote(
                outgo.at[group, target],
                landed.at[group, me],
                send_sems.at[1],
                route_sems.at[group],
                target,
            )
        take(landed, group, me)

    loads[2].wait()

    def adam_block(b, total):
        row_sum = jnp.zeros((8, LANES), jnp.float32)
        for half in range(2):
            for quarter in range(4):
                rows = pl.ds(quarter * 64, 64)
                lanes = pl.ds(half * LANES, LANES)
                direction = grad[b, rows, lanes].astype(jnp.float32) / (
                    jnp.sqrt(second[b, rows, lanes]) + ADAM_EPS
                )
                row_sum += jnp.sum((direction * direction).reshape(8, 8, LANES), axis=0)
        block_sum = jnp.full((1, LANES), jnp.sum(row_sum), jnp.float32)
        norms_ref[b] = block_sum
        return total + block_sum

    sums[N - 1] = lax.fori_loop(0, BLOCKS, adam_block, jnp.zeros((1, LANES), jnp.float32))

    for index, target in enumerate(targets):
        remote(sums.at[N - 1], sums.at[index], send_sems.at[4], sum_sems.at[0], target)

    loads[3].wait()
    loads[4].wait()
    def send_answers(group, core):
        landing = pl.ds(me * CAP + group * PER, PER)
        for target in to_core[core] + ([sibling] if core == 0 else []):
            remote(
                answer.at[group, target],
                arrived.at[landing],
                send_sems.at[2],
                recv_sems.at[1],
                target,
            )
        if core == 0:
            arrived[landing] = answer[group, me]

    for group in range(GROUPS):
        wait_bytes(landed.at[group, pl.ds(0, N - 1)], route_sems.at[group])
        if group > 0:
            send_answers(group - 1, 0)

        def precondition(index, carry):
            slot = group * PER + index
            block = join(lambda k: landed[group, k, index])
            owned[slot] = block
            half_done = jnp.dot(
                left_root[slot], block, preferred_element_type=jnp.float32
            ).astype(jnp.bfloat16)
            full = jnp.dot(
                half_done, right_root[slot], preferred_element_type=jnp.float32
            ).astype(jnp.bfloat16)
            for k in range(N):
                r, half = divmod(k, 2)
                answer[group, k, index] = full[
                    r * ROWS : (r + 1) * ROWS, half * LANES : (half + 1) * LANES
                ]
            return carry

        lax.fori_loop(0, PER, precondition, 0)

    send_answers(GROUPS - 1, 0)
    for group in range(GROUPS):
        send_answers(group, 1)

    wait_bytes(sums.at[pl.ds(0, N - 1)], sum_sems.at[0])
    totals[LAYERS - 1] = jnp.sum(sums[...], axis=0)
    for offset in range(1, LAYERS):
        pltpu.make_async_remote_copy(
            src_ref=totals.at[LAYERS - 1],
            dst_ref=totals.at[offset - 1],
            send_sem=send_sems.at[5],
            recv_sem=sum_sems.at[1],
            device_id={"layer": (layer + offset) % LAYERS},
            device_id_type=MESH,
        ).start()

    wait_bytes(arrived.at[pl.ds(0, CAP * (N - 1))], recv_sems.at[1])

    def give(ref, target):
        for block in range(BLOCKS):
            ref[target, block] = arrived[back_table[0, target * BLOCKS + block]]

    for target in targets:
        give(homing, target)
        remote(homing.at[target], home_ref.at[me], send_sems.at[3], recv_sems.at[2], target)
    give(home_ref, me)

    loads[5].wait()
    loads[6].wait()

    def statistics(slot, carry):
        block = owned[slot]
        gram_left = lax.dot_general(
            block, block, (((1,), (1,)), ((), ())), preferred_element_type=jnp.float32
        )
        gram_right = lax.dot_general(
            block, block, (((0,), (0,)), ((), ())), preferred_element_type=jnp.float32
        )
        new_left_ref[slot] = DECAY_RATE * left_stats[slot] + (1.0 - DECAY_RATE) * gram_left
        new_right_ref[slot] = DECAY_RATE * right_stats[slot] + (1.0 - DECAY_RATE) * gram_right
        return carry

    lax.fori_loop(0, CAP, statistics, 0)


    wait_bytes(totals.at[pl.ds(0, LAYERS - 1)], sum_sems.at[1])
    norms_ref[BLOCKS] = jnp.sum(totals[...], axis=0)
    wait_bytes(leaving.at[pl.ds(0, N - 1)], send_sems.at[0])
    wait_bytes(arrived.at[pl.ds(0, CAP * (N - 1))], send_sems.at[1])
    wait_bytes(arrived.at[pl.ds(0, CAP * (N - 1))], send_sems.at[2])
    wait_bytes(sums.at[pl.ds(0, N - 1)], send_sems.at[4])
    wait_bytes(totals.at[pl.ds(0, LAYERS - 1)], send_sems.at[5])
    wait_bytes(homing.at[pl.ds(0, N - 1)], send_sems.at[3])
    wait_bytes(home_ref.at[pl.ds(0, N - 1)], recv_sems.at[2])


def routed(owner_row, gradients, second_moment, left_root, right_root, left_stats, right_stats):
    bf16, f32 = jnp.bfloat16, jnp.float32
    vmem = pl.BlockSpec(memory_space=pltpu.VMEM)
    hbm = pl.BlockSpec(memory_space=pltpu.HBM)
    operands = [
        pltpu.with_memory_space_constraint(array, pltpu.HBM)
        for array in (
            owner_row, gradients, second_moment, left_root, right_root, left_stats, right_stats
        )
    ]
    return pl.pallas_call(
        routed_kernel,
        out_shape=(
            pltpu.VMEM((CAP, BS, BS), f32),
            pltpu.VMEM((CAP, BS, BS), f32),
            pltpu.VMEM((N, BLOCKS, ROWS, LANES), bf16),
            pltpu.VMEM((BLOCKS + 1, 1, LANES), f32),
        ),
        in_specs=[hbm] * len(operands),
        out_specs=(vmem,) * 4,
        scratch_shapes=[
            pltpu.VMEM((1, NB), jnp.int32),
            pltpu.VMEM((BLOCKS, BS, BS), bf16),
            pltpu.VMEM((BLOCKS, BS, BS), f32),
            pltpu.VMEM((CAP, BS, BS), bf16),
            pltpu.VMEM((CAP, BS, BS), bf16),
            pltpu.VMEM((CAP, BS, BS), f32),
            pltpu.VMEM((CAP, BS, BS), f32),
            pltpu.VMEM((N, BLOCKS, ROWS, LANES), bf16),
            pltpu.VMEM((NB + 1, ROWS, LANES), bf16),
            pltpu.VMEM((GROUPS, N, PER, ROWS, LANES), bf16),
            pltpu.VMEM((GROUPS, N, PER, ROWS, LANES), bf16),
            pltpu.VMEM((CAP, BS, BS), bf16),
            pltpu.VMEM((GROUPS, N, PER, ROWS, LANES), bf16),
            pltpu.VMEM((N * CAP, ROWS, LANES), bf16),
            pltpu.VMEM((N, BLOCKS, ROWS, LANES), bf16),
            pltpu.VMEM((N, 1, LANES), f32),
            pltpu.VMEM((LAYERS, 1, LANES), f32),
            pltpu.VMEM((1, N * CAP), jnp.int32),
            pltpu.VMEM((1, NB), jnp.int32),
            pltpu.SMEM((1, N * CAP), jnp.int32),
            pltpu.SMEM((1, NB), jnp.int32),
            pltpu.SemaphoreType.DMA((7,)),
            pltpu.SemaphoreType.DMA((2,)),
            pltpu.SemaphoreType.DMA((6,)),
            pltpu.SemaphoreType.DMA((GROUPS,)),
            pltpu.SemaphoreType.DMA((3,)),
            pltpu.SemaphoreType.DMA((2,)),
        ],
        compiler_params=pltpu.CompilerParams(
            collective_id=0, has_side_effects=True, vmem_limit_bytes=34 * MIB
        ),
        cost_estimate=pl.CostEstimate(
            flops=4 * 2 * CAP * BS**3, bytes_accessed=18 * MIB, transcendentals=0
        ),
        name="route_blocks",
    )(*operands)


def finish_kernel(left_ref, right_ref, home_ref, norms_ref,
                  update_ref, new_left_ref, new_right_ref, update, sems):
    outs = [
        pltpu.make_async_copy(left_ref, new_left_ref.at[0], sems.at[0]),
        pltpu.make_async_copy(right_ref, new_right_ref.at[0], sems.at[1]),
    ]
    for out in outs:
        out.start()
    entries = float(LAYERS * NB * BS * BS)
    clip_factor = jnp.minimum(1.0, UPDATE_RMS / jnp.sqrt(norms_ref[BLOCKS] / entries))
    for block in range(BLOCKS):
        pre = home_ref[:, block].astype(jnp.float32)
        pre_sq = jnp.full((1, LANES), jnp.sum(pre * pre), jnp.float32)
        ratio = jnp.sqrt(norms_ref[block] / float(BS * BS)) / jnp.sqrt(
            pre_sq / float(BS * BS) + NORM_FLOOR
        )
        factor = ratio * clip_factor
        for k in range(N):
            update[(block,) + piece_place(k)] = (pre[k] * factor).astype(jnp.bfloat16)
    out = pltpu.make_async_copy(update, update_ref.at[0], sems.at[2])
    out.start()
    for copy in outs + [out]:
        copy.wait()


def finish(new_left, new_right, home, norms):
    vmem = pl.BlockSpec(memory_space=pltpu.VMEM)
    hbm = pl.BlockSpec(memory_space=pltpu.HBM)
    return pl.pallas_call(
        finish_kernel,
        out_shape=(
            jax.ShapeDtypeStruct((1, BLOCKS, BS, BS), jnp.bfloat16),
            jax.ShapeDtypeStruct((1, CAP, BS, BS), jnp.float32),
            jax.ShapeDtypeStruct((1, CAP, BS, BS), jnp.float32),
        ),
        in_specs=[vmem] * 4,
        out_specs=(hbm,) * 3,
        scratch_shapes=[
            pltpu.VMEM((BLOCKS, BS, BS), jnp.bfloat16),
            pltpu.SemaphoreType.DMA((3,)),
        ],
        compiler_params=pltpu.CompilerParams(vmem_limit_bytes=8 * MIB),
        cost_estimate=pl.CostEstimate(
            flops=6 * BLOCKS * BS * BS, bytes_accessed=14 * MIB, transcendentals=0
        ),
        name="write_results",
    )(new_left, new_right, home, norms)


def per_device(gradients, second_moment, owners, left_stats, right_stats, left_root, right_root):
    owner_row = owners.reshape(1, NB)
    new_left, new_right, home, norms = routed(
        owner_row, gradients, second_moment, left_root, right_root, left_stats, right_stats
    )
    return finish(new_left, new_right, home, norms)


def solution(mesh):
    blocked = P("layer", "fsdp", None, None)
    return jax.shard_map(
        per_device,
        mesh=mesh,
        in_specs=(blocked, blocked, P("layer", None, None), blocked, blocked, blocked, blocked),
        out_specs=(blocked, blocked, blocked),
        check_vma=False,
    )
```
